32 devices in a mesh: slides: 2 (over x), seq: 16 (over z, y, core).
Axes of the slice: x: 2, y: 2, z: 4, core: 2. Of those that a mesh axis runs over, the one named last changes fastest.
Arguments:
- queries: bfloat16 [16384, 768], P(('slides', 'seq')), parts along dimension 0, may hold values from -72 to 72
- key_rows: bfloat16 [16384, 768], P(('slides', 'seq')), parts along dimension 0, may hold values from -6 to 6
- value_rows: bfloat16 [16384, 768], P(('slides', 'seq')), parts along dimension 0, may hold values from -6 to 6
- offsets: int32 [3, 16], replicated, may hold values from 0 to 15, as said below
Outputs:
- attended: bfloat16 [16384, 768], P(('slides', 'seq')), parts along dimension 0
The draws below stay inside these ranges and needn't reach their ends.
There are 2 independent parts, one for each index of `slides`. The reference program is written for one: setup_inputs(seed, part) draws one part's arguments, and reference() takes and returns one part's arrays. A program takes and returns all parts, laid end to end along the dimension named above; an argument that names none is the same for every part. Nothing has to cross between parts.
Inputs may be any that keep to these rules, and one draw needn't show every extreme that they name: offsets[0, h] is below 4, offsets[1, h] below 16, offsets[2, h] below 16; some head has offset 16 - 1 at the widest scale.
All inputs are finite; a program needn't handle non-finite values.
Results may differ from the reference program's by a relative error of at most 0.0045.
Values may be sent and summed in bfloat16 or wider, within the bound.
No kernel may reach another device: no remote copies, remote signals or barrier semaphores. Data moves between devices by JAX's collectives and lax.ppermute only.
A program may use at most 128 MiB of HBM per device.

```python
import jax
import jax.numpy as jnp
from jax import lax

H = 16
HD = 48
D = 768
TOK_DEV = 512
NEAR_SPAN = 4
MID_SPAN = 16
TOKENS = 8192
N_SEQ = 16


def normal_base(key):
    return jnp.clip(jax.random.normal(key, (TOKENS, D), jnp.float32), -6.0, 6.0)


def draw_key_rows(key, part):
    shared = normal_base(key)
    return shared.astype(jnp.bfloat16)


def draw_queries(key, part):
    key = jax.random.fold_in(key, 11)
    result = normal_base(key)
    return result.astype(jnp.bfloat16)


def draw_offsets(key, part):
    key = jax.random.fold_in(key, 23)
    first_key, second_key = jax.random.split(key)
    limits = jnp.array([[NEAR_SPAN], [MID_SPAN], [N_SEQ]], jnp.int32)
    drawn = jax.random.randint(first_key, (3, H), 0, limits, jnp.int32)
    chosen = jax.random.randint(second_key, (), 0, H, jnp.int32)
    heads = jnp.arange(H, dtype=jnp.int32)[None, :]
    levels = jnp.arange(3, dtype=jnp.int32)[:, None]
    drawn = jnp.where(heads == chosen, limits - 1, drawn)
    drawn = jnp.where((levels == 0) & (heads == (chosen + 1) % H), 0, drawn)
    return drawn.astype(jnp.int32)


def level_of(key, dims, cuts, low, top_value):
    def one(dim, parts):
        heights = jax.random.uniform(jax.random.fold_in(jax.random.fold_in(key, 6), dim), (parts,), jnp.float32, low / len(cuts), top_value / len(cuts))
        return jnp.repeat(jnp.exp(heights), dims[dim] // parts).reshape((-1,) + (1,) * (len(dims) - dim - 1))

    level = one(*cuts[0])
    for cut in cuts[1:]:
        level = level * one(*cut)
    return level


def centred(rng, extent, spread, most, pieces=(), held_as=jnp.bfloat16):
    values = spread * jax.random.normal(rng, extent, jnp.float32)
    if pieces:
        values = values * level_of(rng, extent, pieces, -0.22, 0.18)
    return jnp.clip(values, -most, most).astype(held_as)


def setup_inputs(seed: int = 0, part: int = 0) -> dict:
    streams_of = jax.random.split(jax.random.key(seed), 5)
    part_splits = jax.random.split(jax.random.fold_in(streams_of[4], part), 5)
    return {
        "queries": draw_queries(jax.random.fold_in(jax.random.fold_in(streams_of[4], part), 71), part),
        "key_rows": draw_key_rows(jax.random.fold_in(jax.random.fold_in(streams_of[4], part), 71), part),
        "value_rows": centred(part_splits[2], (TOKENS, D), 1.0, 6.0, ((0, 16),)),
        "offsets": draw_offsets(jax.random.fold_in(streams_of[4], 71), part),
    }


def attend(block_q, block_k, block_v):
    scores = jnp.einsum("qhd,khd->hqk", block_q.astype(jnp.float32), block_k.astype(jnp.float32)) * (HD ** -0.5)
    top = jnp.max(scores, axis=-1, keepdims=True)
    expo = jnp.exp(scores - top)
    total = jnp.sum(expo, axis=-1)
    probs = expo.astype(jnp.bfloat16)
    mixed = jnp.einsum("hqk,khd->qhd", probs.astype(jnp.float32), block_v.astype(jnp.float32))
    mixed = mixed / jnp.transpose(total)[:, :, None]
    return mixed, jnp.transpose(top[..., 0] + jnp.log(total))


def scale_terms(query_all, key_all, value_all, choose, span, dilation):
    count = TOKENS // span
    inner = span // dilation

    def select(data):
        shaped = data.reshape(count, inner, dilation, H, HD)
        return jnp.take_along_axis(shaped, choose[None, None, None, :, None], axis=2)[:, :, 0]

    mixed, spread_lse = lax.map(lambda group: attend(group[0], group[1], group[2]), (select(query_all), select(key_all), select(value_all)))
    selected = jnp.arange(dilation)[:, None] == choose[None, :]
    full_mixed = jnp.where(selected[None, None, :, :, None], mixed[:, :, None], jnp.float32(0.0)).reshape(TOKENS, H, HD)
    full_lse = jnp.where(selected[None, None], spread_lse[:, :, None], jnp.float32(-1e30)).reshape(TOKENS, H)
    return full_mixed, full_lse


def reference(queries, key_rows, value_rows, offsets):
    query_all = queries.reshape(TOKENS, H, HD)
    key_all = key_rows.reshape(TOKENS, H, HD)
    value_all = value_rows.reshape(TOKENS, H, HD)
    plans = [(TOK_DEV, 1, jnp.zeros((H,), jnp.int32)), (NEAR_SPAN * TOK_DEV, NEAR_SPAN, offsets[0]), (MID_SPAN * TOK_DEV, MID_SPAN, offsets[1]), (TOKENS, N_SEQ, offsets[2])]
    outputs = [scale_terms(query_all, key_all, value_all, plan[2], plan[0], plan[1]) for plan in plans]
    highest = outputs[0][1]
    for entry in outputs[1:]:
        highest = jnp.maximum(highest, entry[1])
    numer = jnp.zeros((TOKENS, H, HD), jnp.float32)
    denom = jnp.zeros((TOKENS, H), jnp.float32)
    for entry in outputs:
        weight = jnp.exp(entry[1] - highest)
        denom = denom + weight
        numer = numer + weight[:, :, None] * entry[0]
    return (numer / denom[:, :, None]).reshape(TOKENS, D).astype(jnp.bfloat16)
```

```python
import functools

import jax
import jax.numpy as jnp
from jax import lax
from jax.experimental import pallas as pl
from jax.experimental.pallas import tpu as pltpu
from jax.sharding import PartitionSpec as P

H = 16
HD = 48
D = 768
NEAR_SPAN = 4
MID_SPAN = 16
HALF = 384
TILE = 128
SCALE = HD ** (-0.5)
LOG2E = 1.4426950408889634
VMEM_BYTES = 48 * 1024 * 1024
BF = jnp.bfloat16
F32 = jnp.float32


def from_partner(block, axis, flip):
    count = lax.axis_size(axis)
    return lax.ppermute(block, axis, [(i, i ^ flip) for i in range(count)])


def params():
    return pltpu.CompilerParams(vmem_limit_bytes=VMEM_BYTES)


def cost(flops, moved, exps=0):
    return pl.CostEstimate(flops=flops, bytes_accessed=moved, transcendentals=exps)


def stride_matrix(rows, inverse):
    groups = rows // MID_SPAN
    row = lax.broadcasted_iota(jnp.int32, (rows, 1), 0)
    col = lax.broadcasted_iota(jnp.int32, (rows, rows), 1)
    if inverse:
        target = (row % MID_SPAN) * groups + row // MID_SPAN
    else:
        target = (row % groups) * MID_SPAN + row // groups
    return jnp.where(col == target, F32(1.0), F32(0.0)).astype(BF)


def lane_offsets(offsets_ref, scale):
    head = lax.broadcasted_iota(jnp.int32, (1, D), 1) // HD
    result = jnp.zeros((1, D), jnp.int32)
    for h in range(H):
        result = jnp.where(head == h, offsets_ref[scale, h], result)
    return result


def pick(blocks, hits):
    result = blocks[0]
    for block, hit in zip(blocks[1:], hits[1:]):
        result = jnp.where(hit, block, result)
    return result


def prep_kernel(wide, offsets_ref, q_ref, k_ref, v_ref, strided_ref, near_q_ref, near_kv_ref, send_ref):
    rows = q_ref.shape[0]
    groups = rows // MID_SPAN
    matrix = stride_matrix(rows, False)
    offs = [lane_offsets(offsets_ref, s) for s in range(1 + wide)]
    near_hits = [offs[0] == b for b in range(NEAR_SPAN)]
    wide_hits = [[offs[1 + s] == o for o in range(MID_SPAN)] for s in range(wide)]
    chunks = [[] for _ in range(H)]
    for index, ref in enumerate((q_ref, k_ref, v_ref)):
        moved = jnp.dot(matrix, ref[...], preferred_element_type=F32)
        if index == 0:
            strided_ref[...] = moved.astype(BF)
        block = [moved[o * groups : (o + 1) * groups] for o in range(MID_SPAN)]
        for a in range(NEAR_SPAN):
            part = pick(block[a * NEAR_SPAN : (a + 1) * NEAR_SPAN], near_hits).astype(BF)
            if index == 0:
                near_q_ref[a * groups : (a + 1) * groups, :] = part
            else:
                base = (index - 1) * rows // NEAR_SPAN + a * groups
                near_kv_ref[base : base + groups, :] = part
        for s in range(wide):
            chosen = pick(block, wide_hits[s])
            for g in range(groups // 16):
                for h in range(H):
                    chunks[h].append(chosen[g * 16 : (g + 1) * 16, h * HD : (h + 1) * HD])
    lanes = send_ref.shape[1]
    for h in range(H):
        spare = lanes - len(chunks[h]) * HD
        if spare:
            chunks[h].append(jnp.zeros((16, spare), F32))
        send_ref[h * 16 : (h + 1) * 16, :] = jnp.concatenate(chunks[h], axis=1).astype(BF)


def probabilities(scores):
    top = jnp.max(scores, axis=1, keepdims=True)
    return jnp.exp2((scores - top) * F32(SCALE * LOG2E)).astype(BF), top


def attend_half(q, k, v):
    count = q.shape[0]
    lane = lax.broadcasted_iota(jnp.int32, (1, TILE), 1)
    wide_lane = lax.broadcasted_iota(jnp.int32, (1, 2 * TILE), 1)
    num = [None] * 3
    den = [None] * 3
    top_tiles = [jnp.zeros((count, TILE), F32) for _ in range(3)]

    def add(into, tile, value):
        into[tile] = value if into[tile] is None else into[tile] + value

    for h in range(HALF // HD):
        low, high = h * HD, (h + 1) * HD
        start = 0 if high <= 2 * TILE else TILE
        window = slice(start, start + 2 * TILE)
        inside = (wide_lane >= low - start) & (wide_lane < high - start)
        mask = jnp.where(inside, F32(1.0), F32(0.0)).astype(BF)
        scores = lax.dot_general(
            q[:, window] * mask, k[:, window], (((1,), (1,)), ((), ())), preferred_element_type=F32
        )
        probs, top = probabilities(scores)
        first, last = low // TILE, (high - 1) // TILE
        inside_first = (lane >= low - first * TILE) & (lane < high - first * TILE)
        ones_first = jnp.where(inside_first, F32(1.0), F32(0.0)).astype(BF)
        v_first = v[:, first * TILE : (first + 1) * TILE] * ones_first
        if first == last:
            weights = jnp.concatenate([v_first, jnp.broadcast_to(ones_first, v_first.shape)], axis=1)
            result = jnp.dot(probs, weights, preferred_element_type=F32)
            add(num, first, result[:, :TILE])
            add(den, first, result[:, TILE:])
            top_tiles[first] = jnp.where(inside_first, top, top_tiles[first])
        else:
            inside_last = lane < high - last * TILE
            ones_last = jnp.where(inside_last, F32(1.0), F32(0.0)).astype(BF)
            v_last = v[:, last * TILE : (last + 1) * TILE] * ones_last
            weights = jnp.concatenate([v_first + ones_last, v_last + ones_first], axis=1)
            result = jnp.dot(probs, weights, preferred_element_type=F32)
            left, right = result[:, :TILE], result[:, TILE:]
            zero = F32(0.0)
            add(num, first, jnp.where(inside_first, left, zero))
            add(den, first, jnp.where(inside_first, right, zero))
            add(num, last, jnp.where(inside_last, right, zero))
            add(den, last, jnp.where(inside_last, left, zero))
            top_tiles[first] = jnp.where(inside_first, top, top_tiles[first])
            top_tiles[last] = jnp.where(inside_last, top, top_tiles[last])
    branch = [n / d for n, d in zip(num, den)]
    lse = [t * F32(SCALE) + jnp.log(d) for t, d in zip(top_tiles, den)]
    return branch, lse


def store_tiles(ref, tiles):
    for t, tile in enumerate(tiles):
        ref[:, t * TILE : (t + 1) * TILE] = tile


def local_kernel(q_ref, k_ref, v_ref, branch_ref, lse_ref):
    branch, lse = attend_half(q_ref[...], k_ref[...], v_ref[...])
    store_tiles(branch_ref, branch)
    store_tiles(lse_ref, lse)


def near_kernel(q_ref, *refs):
    kv_refs, (branch_ref, lse_ref) = refs[:NEAR_SPAN], refs[NEAR_SPAN:]
    half = kv_refs[0].shape[0] // 2
    keys = jnp.concatenate([ref[:half, :] for ref in kv_refs], axis=0)
    values = jnp.concatenate([ref[half:, :] for ref in kv_refs], axis=0)
    branch, lse = attend_half(q_ref[...], keys, values)
    store_tiles(branch_ref, branch)
    store_tiles(lse_ref, lse)


def owned_kernel(wide, recv_ref, back_ref):
    everything = recv_ref[...].astype(F32)
    parts = 2
    pieces = []

    def rows_of(x, s):
        found = []
        for g in range(parts):
            c = (x * wide + s) * parts + g
            found.append(everything[:, c * HD : (c + 1) * HD])
        return jnp.concatenate(found, axis=0).astype(BF)

    stats = []
    for s in range(wide):
        q, k, v = (rows_of(x, s) for x in range(3))
        scores = lax.dot_general(q, k, (((1,), (1,)), ((), ())), preferred_element_type=F32)
        probs, top = probabilities(scores)
        weights = jnp.concatenate([v, jnp.ones((v.shape[0], TILE - HD), BF)], axis=1)
        result = jnp.dot(probs, weights, preferred_element_type=F32)
        total = result[:, HD : HD + 1]
        branch = result[:, :HD] / total
        lse = top * F32(SCALE) + jnp.log(total)
        first = lse.astype(BF).astype(F32)
        second = (lse - first).astype(BF).astype(F32)
        third = lse - first - second
        half = branch.shape[0] // parts
        for g in range(parts):
            rows = slice(g * half, (g + 1) * half)
            pieces.append(branch[rows])
            stats += [first[rows], second[rows], third[rows]]
    pieces += stats
    used = sum(piece.shape[1] for piece in pieces)
    pieces.append(jnp.zeros((pieces[0].shape[0], back_ref.shape[1] - used), F32))
    back_ref[...] = jnp.concatenate(pieces, axis=1).astype(BF)


def combine(branch_a, lse_a, branch_b, lse_b):
    high = jnp.maximum(lse_a, lse_b)
    weight_a = jnp.exp(lse_a - high)
    weight_b = jnp.exp(lse_b - high)
    total = weight_a + weight_b
    return (weight_a * branch_a + weight_b * branch_b) / total, high + jnp.log(total)


def merge_kernel(wide, dense, offsets_ref, branch_ref, lse_ref, near_branch_ref, near_lse_ref, back_ref, *refs):
    out_ref = refs[-1]
    rows = out_ref.shape[0]
    groups = rows // MID_SPAN
    parts = groups // 16
    spans = [slice(o * groups, (o + 1) * groups) for o in range(MID_SPAN)]
    branch = [branch_ref[span, :] for span in spans]
    lse = [lse_ref[span, :] for span in spans]

    def fold(members, hits, other_branch, other_lse):
        mixed, high = combine(
            pick([branch[o] for o in members], hits),
            pick([lse[o] for o in members], hits),
            other_branch,
            other_lse,
        )
        for o, hit in zip(members, hits):
            branch[o] = jnp.where(hit, mixed, branch[o])
            lse[o] = jnp.where(hit, high, lse[o])

    near = lane_offsets(offsets_ref, 0)
    near_hits = [near == b for b in range(NEAR_SPAN)]
    for a in range(NEAR_SPAN):
        span = slice(a * groups, (a + 1) * groups)
        members = range(a * NEAR_SPAN, (a + 1) * NEAR_SPAN)
        fold(members, near_hits, near_branch_ref[span, :], near_lse_ref[span, :])
    back = back_ref[...].astype(F32)
    for s in range(wide):
        wide_branch, wide_lse = [], []
        for g in range(parts):
            c = s * parts + g
            at = wide * parts * HD + 3 * c
            total = back[:, at : at + 1] + back[:, at + 1 : at + 2] + back[:, at + 2 : at + 3]
            heads = [slice(h * 16, (h + 1) * 16) for h in range(H)]
            wide_branch.append(jnp.concatenate([back[rows_h, c * HD : (c + 1) * HD] for rows_h in heads], axis=1))
            wide_lse.append(jnp.concatenate([jnp.broadcast_to(total[rows_h], (16, HD)) for rows_h in heads], axis=1))
        offs = lane_offsets(offsets_ref, 1 + s)
        hits = [offs == o for o in range(MID_SPAN)]
        fold(range(MID_SPAN), hits, jnp.concatenate(wide_branch, axis=0), jnp.concatenate(wide_lse, axis=0))
    if dense:
        for o, span in enumerate(spans):
            branch[o], lse[o] = combine(branch[o], lse[o], refs[0][span, :], refs[1][span, :])
    final = jnp.concatenate([part.astype(BF) for part in branch], axis=0)
    moved = jnp.dot(stride_matrix(rows, True), final, preferred_element_type=F32)
    out_ref[...] = moved.astype(BF)


def vmem(count):
    return [pl.BlockSpec(memory_space=pltpu.VMEM)] * count


def far_by_gather(queries, key_rows, value_rows, choose, dilation):
    rows = queries.shape[0]

    def select(data):
        shaped = data.reshape(rows // dilation, dilation, H, HD)
        return jnp.take_along_axis(shaped, choose[None, None, :, None], axis=1)[:, 0]

    def gathered(data):
        flat = lax.all_gather(select(data).reshape(-1, D), "seq", axis=0, tiled=True)
        return flat.reshape(-1, H, HD)

    keys, values = gathered(key_rows), gathered(value_rows)
    scores = jnp.einsum("qhd,khd->hqk", select(queries), keys, preferred_element_type=F32) * SCALE
    top = jnp.max(scores, axis=-1, keepdims=True)
    expo = jnp.exp(scores - top)
    total = jnp.sum(expo, axis=-1)
    mixed = jnp.einsum("hqk,khd->qhd", expo.astype(BF), values, preferred_element_type=F32)
    mixed = mixed / jnp.transpose(total)[:, :, None]
    lse = jnp.transpose(top[..., 0] + jnp.log(total))
    selected = jnp.arange(dilation)[:, None] == choose[None, :]
    full_mixed = jnp.where(selected[None, :, :, None], mixed[:, None], F32(0.0)).reshape(rows, D)
    full_lse = jnp.where(selected[None], lse[:, None], F32(-1e30)).reshape(rows, H)
    full_lse = jnp.repeat(full_lse, HD, axis=1)

    def strided(data):
        return data.reshape(rows // MID_SPAN, MID_SPAN, D).swapaxes(0, 1).reshape(rows, D)

    return strided(full_mixed), strided(full_lse)


def exchange(blocks):
    count = lax.axis_size("seq")
    teams = None
    if count != MID_SPAN:
        teams = [[first + i for i in range(MID_SPAN)] for first in range(0, count, MID_SPAN)]
    return lax.all_to_all(blocks, "seq", 0, 0, axis_index_groups=teams, tiled=True)


def padded(lanes):
    return -(-lanes // TILE) * TILE


def shards(queries, key_rows, value_rows, offsets):
    rows = queries.shape[0]
    count = lax.axis_size("seq")
    wide = 2 if count == MID_SPAN else 1
    parts = rows // MID_SPAN // 16
    near_rows = rows // NEAR_SPAN
    send_lanes = padded(3 * wide * parts * HD)
    back_lanes = padded(wide * parts * (HD + 3))
    smem = pl.BlockSpec(memory_space=pltpu.SMEM)
    shape = jax.ShapeDtypeStruct

    strided_q, near_q, near_kv, send = pl.pallas_call(
        functools.partial(prep_kernel, wide),
        out_shape=(
            shape((rows, D), BF),
            shape((near_rows, D), BF),
            shape((2 * near_rows, D), BF),
            shape((H * 16, send_lanes), BF),
        ),
        in_specs=[smem] + vmem(3),
        out_specs=tuple(vmem(4)),
        compiler_params=params(),
        cost_estimate=cost(6 * rows * rows * D, 10 * rows * D),
        name="prep",
    )(offsets, queries, key_rows, value_rows)

    recv = exchange(send)
    near_core = from_partner(near_kv, "seq", 1)
    near_side = from_partner(near_kv, "seq", 2)
    near_both = from_partner(near_side, "seq", 1)

    half = lambda height: pl.BlockSpec((height, HALF), lambda i: (0, i))
    branch, lse = pl.pallas_call(
        local_kernel,
        grid=(D // HALF,),
        out_shape=(shape((rows, D), F32), shape((rows, D), F32)),
        in_specs=[half(rows)] * 3,
        out_specs=(half(rows), half(rows)),
        compiler_params=params(),
        cost_estimate=cost(4 * rows * rows * H * 256, 14 * rows * D, rows * rows * H),
        name="local",
    )(strided_q, key_rows, value_rows)

    back = exchange(
        pl.pallas_call(
            functools.partial(owned_kernel, wide),
            out_shape=shape((H * 16, back_lanes), BF),
            in_specs=vmem(1),
            out_specs=vmem(1)[0],
            compiler_params=params(),
            cost_estimate=cost(4 * wide * rows * rows * 256, 4 * 256 * send_lanes, wide * rows * rows),
            name="owned",
        )(recv)
    )

    near_branch, near_lse = pl.pallas_call(
        near_kernel,
        grid=(D // HALF,),
        out_shape=(shape((near_rows, D), F32), shape((near_rows, D), F32)),
        in_specs=[half(near_rows)] + [half(2 * near_rows)] * NEAR_SPAN,
        out_specs=(half(near_rows), half(near_rows)),
        compiler_params=params(),
        cost_estimate=cost(4 * near_rows * rows * H * 256, 8 * rows * D, near_rows * rows * H),
        name="near",
    )(near_q, near_kv, near_core, near_side, near_both)

    extra = []
    if wide == 1:
        extra = list(far_by_gather(queries, key_rows, value_rows, offsets[2], count))
    return pl.pallas_call(
        functools.partial(merge_kernel, wide, bool(extra)),
        out_shape=shape((rows, D), BF),
        in_specs=[smem] + vmem(5 + len(extra)),
        out_specs=vmem(1)[0],
        compiler_params=params(),
        cost_estimate=cost(2 * rows * rows * D, 14 * rows * D),
        name="merge",
    )(offsets, branch, lse, near_branch, near_lse, back, *extra)


def solution(mesh):
    in_specs = (
        P(("slides", "seq"), None),
        P(("slides", "seq"), None),
        P(("slides", "seq"), None),
        P(),
    )
    out_specs = P(("slides", "seq"), None)
    return jax.shard_map(shards, mesh=mesh, in_specs=in_specs, out_specs=out_specs, check_vma=False)
```

```python
import functools

import jax
import jax.numpy as jnp
from jax import lax
from jax.experimental import pallas as pl
from jax.experimental.pallas import tpu as pltpu
from jax.sharding import PartitionSpec as P

H = 16
HD = 48
D = 768
NEAR_SPAN = 4
MID_SPAN = 16
HALF = 384
TILE = 128
HALF_HEADS = HALF // HD
PARTS = D // HALF
PART_TILES = HALF // TILE
STAT_LANE = (2 * HD, 2 * HD + 16)
SCALE = HD ** (-0.5)
LOG2E = 1.4426950408889634
VMEM_BYTES = 63 * 1024 * 1024
SMALL_BYTES = 48 * 1024 * 1024
OWNED_BYTES = 32 * 1024 * 1024
BF = jnp.bfloat16
F32 = jnp.float32


def from_partner(block, axis, flip):
    count = lax.axis_size(axis)
    return lax.ppermute(block, axis, [(i, i ^ flip) for i in range(count)])


def params(limit=VMEM_BYTES):
    return pltpu.CompilerParams(vmem_limit_bytes=limit)


def cost(flops, moved, exps=0):
    return pl.CostEstimate(flops=flops, bytes_accessed=moved, transcendentals=exps)


def tile_offsets(offsets_ref, scale, tile, rows):
    lane = lax.broadcasted_iota(jnp.int32, (rows, TILE), 1)
    heads = list(heads_of(tile))
    result = jnp.full((rows, TILE), offsets_ref[scale, heads[0]], jnp.int32)
    for h in heads[1:]:
        result = jnp.where(lane >= h * HD - tile * TILE, offsets_ref[scale, h], result)
    return result


def inside(lane, low, high):
    return jnp.where((lane >= low) & (lane < high), F32(1.0), F32(0.0)).astype(BF)


def heads_of(tile):
    return range(tile * TILE // HD, ((tile + 1) * TILE - 1) // HD + 1)


def tiles_of(head):
    return range(head * HD // TILE, ((head + 1) * HD - 1) // TILE + 1)


def every(first, rows):
    return pl.ds(first, rows // MID_SPAN, stride=MID_SPAN)


def bits_of(offs, count):
    return [(offs & (1 << k)) != 0 for k in range(count.bit_length() - 1)]


def pick(blocks, bits):
    for bit in bits:
        blocks = [jnp.where(bit, high, low) for low, high in zip(blocks[::2], blocks[1::2])]
    return blocks[0]


def lanes_of(part):
    return slice(part * HALF, (part + 1) * HALF)


def flights(pairs, sems):
    copies = [pltpu.make_async_copy(src, dst, sems.at[i]) for i, (src, dst) in enumerate(pairs)]
    for copy in copies:
        copy.start()
    return copies


def scale_lane(scale):
    return scale * HD


def prep_kernel(
    wide, offsets_ref, q_ref, k_ref, v_ref, near_q_out, near_out, send_out,
    stage, single, near_q, near, send, in_sems, out_sems,
):
    rows = q_ref.shape[0]
    groups = rows // MID_SPAN
    near_rows = rows // NEAR_SPAN
    arrivals = flights(
        [
            (ref.at[:, lanes_of(part)], stage.at[x, :, lanes_of(part)])
            for part in range(PARTS)
            for x, ref in enumerate((q_ref, k_ref, v_ref))
        ],
        in_sems,
    )
    lane = lax.broadcasted_iota(jnp.int32, (groups, TILE), 1)
    leaving = []
    for part in range(PARTS):
        here = lanes_of(part)
        tiles = range(part * PART_TILES, (part + 1) * PART_TILES)
        bits = [
            {t: bits_of(tile_offsets(offsets_ref, s, t, groups), MID_SPAN if s else NEAR_SPAN) for t in tiles}
            for s in range(1 + wide)
        ]
        for x in range(3):
            arrivals[part * 3 + x].wait()
            chosen = [{} for _ in range(wide)]
            for t in tiles:
                lanes = slice(t * TILE, (t + 1) * TILE)
                single[x, t] = stage[x, :, lanes].astype(F32)
                block = [single[x, t, every(o, rows), :] for o in range(MID_SPAN)]
                for a in range(NEAR_SPAN):
                    picked = pick(block[a * NEAR_SPAN : (a + 1) * NEAR_SPAN], bits[0][t]).astype(BF)
                    if x == 0:
                        near_q[a * groups : (a + 1) * groups, lanes] = picked
                    else:
                        base = (x - 1) * near_rows + a * groups
                        near[base : base + groups, lanes] = picked
                for s in range(wide):
                    picked = pick(block, bits[1 + s][t])
                    chosen[s][t] = pltpu.roll(picked, scale_lane(s), 1) if s else picked
            for h in range(part * HALF_HEADS, (part + 1) * HALF_HEADS):
                travel = jnp.zeros((groups, TILE), F32)
                for s in range(wide):
                    for t in tiles_of(h):
                        low, high = max(h * HD, t * TILE), min((h + 1) * HD, (t + 1) * TILE)
                        turned = (lane - scale_lane(s)) & (TILE - 1)
                        hit = (turned >= low - t * TILE) & (turned < high - t * TILE)
                        travel = jnp.where(hit, chosen[s][t], travel)
                send[h * 3 * groups + x * groups : h * 3 * groups + (x + 1) * groups, :] = travel.astype(BF)
        owners = slice(part * HALF_HEADS * 3 * groups, (part + 1) * HALF_HEADS * 3 * groups)
        leaving += flights(
            [
                (send.at[owners], send_out.at[owners]),
                (near.at[:, here], near_out.at[:, here]),
                (near_q.at[:, here], near_q_out.at[:, here]),
            ],
            out_sems.at[part],
        )
    for copy in leaving:
        copy.wait()


def probabilities(scores):
    top = jnp.max(scores, axis=1, keepdims=True)
    return jnp.exp2((scores - top) * F32(SCALE * LOG2E)).astype(BF), top


def attend_half(q, k, v, stacked):
    count = q.shape[0]
    lane = lax.broadcasted_iota(jnp.int32, (1, TILE), 1)
    full_lane = lax.broadcasted_iota(jnp.int32, (count, TILE), 1)
    wide_lane = lax.broadcasted_iota(jnp.int32, (1, 2 * TILE), 1)
    num = [None] * 3
    den = [None] * 3
    top_tiles = [jnp.zeros((count, TILE), F32) for _ in range(3)]

    def add(into, tile, value):
        into[tile] = value if into[tile] is None else into[tile] + value

    def masked_query(h, start):
        return q[:, start : start + 2 * TILE] * inside(wide_lane, h * HD - start, (h + 1) * HD - start)

    def scores_of(left, start):
        right = k[:, start : start + 2 * TILE]
        return lax.dot_general(left, right, (((1,), (1,)), ((), ())), preferred_element_type=F32)

    starts = [0 if (h + 1) * HD <= 2 * TILE else TILE for h in range(HALF_HEADS)]
    ready = {}
    if stacked:
        for start in (0, TILE):
            members = [h for h in range(HALF_HEADS) if starts[h] == start]
            together = scores_of(jnp.concatenate([masked_query(h, start) for h in members], axis=0), start)
            for i, h in enumerate(members):
                ready[h] = together[i * count : (i + 1) * count]
    for h in range(HALF_HEADS):
        low, high = h * HD, (h + 1) * HD
        scores = ready[h] if stacked else scores_of(masked_query(h, starts[h]), starts[h])
        probs, top = probabilities(scores)
        first, last = low // TILE, (high - 1) // TILE
        inside_first = (full_lane >= low - first * TILE) & (full_lane < high - first * TILE)
        ones_first = inside(lane, low - first * TILE, high - first * TILE)
        v_first = v[:, first * TILE : (first + 1) * TILE] * ones_first
        if first == last:
            weights = jnp.concatenate([v_first, jnp.broadcast_to(ones_first, v_first.shape)], axis=1)
            result = jnp.dot(probs, weights, preferred_element_type=F32)
            add(num, first, result[:, :TILE])
            add(den, first, result[:, TILE:])
            top_tiles[first] = jnp.where(inside_first, top, top_tiles[first])
        else:
            inside_last = full_lane < high - last * TILE
            ones_last = inside(lane, 0, high - last * TILE)
            v_last = v[:, last * TILE : (last + 1) * TILE] * ones_last
            weights = jnp.concatenate([v_first + ones_last, v_last + ones_first], axis=1)
            result = jnp.dot(probs, weights, preferred_element_type=F32)
            left, right = result[:, :TILE], result[:, TILE:]
            zero = F32(0.0)
            add(num, first, jnp.where(inside_first, left, zero))
            add(den, first, jnp.where(inside_first, right, zero))
            add(num, last, jnp.where(inside_last, right, zero))
            add(den, last, jnp.where(inside_last, left, zero))
            top_tiles[first] = jnp.where(inside_first, top, top_tiles[first])
            top_tiles[last] = jnp.where(inside_last, top, top_tiles[last])
    branch = [n / d for n, d in zip(num, den)]
    lse = [t * F32(SCALE) + jnp.log(d) for t, d in zip(top_tiles, den)]
    return branch, lse


def local_kernel(q_ref, k_ref, v_ref, own_out, stage, own, in_sems, out_sems):
    arrivals = flights(
        [
            (ref.at[:, lanes_of(part)], stage.at[x, :, lanes_of(part)])
            for part in range(PARTS)
            for x, ref in enumerate((q_ref, k_ref, v_ref))
        ],
        in_sems,
    )
    leaving = []
    for part in range(PARTS):
        here = lanes_of(part)
        for x in range(3):
            arrivals[part * 3 + x].wait()
        branch_tiles, lse_tiles = attend_half(stage[0, :, here], stage[1, :, here], stage[2, :, here], False)
        for t in range(PART_TILES):
            own[0, part * PART_TILES + t] = branch_tiles[t]
            own[1, part * PART_TILES + t] = lse_tiles[t]
        tiles = range(part * PART_TILES, (part + 1) * PART_TILES)
        leaving += flights([(own.at[i, t], own_out.at[i, t]) for i in range(2) for t in tiles], out_sems.at[part])
    for copy in leaving:
        copy.wait()


def combine(branch_a, lse_a, branch_b, lse_b):
    high = jnp.maximum(lse_a, lse_b)
    weight_a = jnp.exp(lse_a - high)
    weight_b = jnp.exp(lse_b - high)
    total = weight_a + weight_b
    return (weight_a * branch_a + weight_b * branch_b) / total, high + jnp.log(total)


def near_kernel(wide, offsets_ref, q_ref, *refs):
    kv_refs, (own_ref, state_out) = refs[:NEAR_SPAN], refs[NEAR_SPAN : NEAR_SPAN + 2]
    q_stage, kv_stage, own, picked, kv_sems, own_sems, out_sems = refs[NEAR_SPAN + 2 :]
    near_rows = q_ref.shape[0]
    rows = own_ref.shape[2]
    groups = rows // MID_SPAN
    arrivals, own_arrivals, leaving = [], [], []
    for part in range(PARTS):
        here = lanes_of(part)
        pairs = [(q_ref.at[:, here], q_stage.at[:, here])]
        for i, ref in enumerate(kv_refs):
            for x in range(2):
                rows_x = slice(x * near_rows, (x + 1) * near_rows)
                rows_i = slice(i * near_rows, (i + 1) * near_rows)
                pairs.append((ref.at[rows_x, here], kv_stage.at[x, rows_i, here]))
        arrivals.append(flights(pairs, kv_sems.at[part]))
        tiles = range(part * PART_TILES, (part + 1) * PART_TILES)
        own_arrivals.append(
            flights([(own_ref.at[i, t], own.at[i, t]) for i in range(2) for t in tiles], own_sems.at[part])
        )
    for part in range(PARTS):
        here = lanes_of(part)
        for copy in arrivals[part]:
            copy.wait()
        near_branch, near_lse = attend_half(q_stage[:, here], kv_stage[0, :, here], kv_stage[1, :, here], True)
        for copy in own_arrivals[part]:
            copy.wait()
        for i in range(PART_TILES):
            t = part * PART_TILES + i
            branch = [own[0, t, every(o, rows), :] for o in range(MID_SPAN)]
            lse = [own[1, t, every(o, rows), :] for o in range(MID_SPAN)]
            offs = tile_offsets(offsets_ref, 0, t, groups)
            hits, bits = [offs == b for b in range(NEAR_SPAN)], bits_of(offs, NEAR_SPAN)
            for a in range(NEAR_SPAN):
                members = slice(a * NEAR_SPAN, (a + 1) * NEAR_SPAN)
                span = slice(a * groups, (a + 1) * groups)
                mixed, high = combine(
                    pick(branch[members], bits), pick(lse[members], bits), near_branch[i][span], near_lse[i][span]
                )
                for b, hit in enumerate(hits):
                    o = a * NEAR_SPAN + b
                    branch[o] = jnp.where(hit, mixed, branch[o])
                    lse[o] = jnp.where(hit, high, lse[o])
            for o in range(MID_SPAN):
                own[0, t, every(o, rows), :] = branch[o]
            for s in range(wide):
                bits = bits_of(tile_offsets(offsets_ref, 1 + s, t, groups), MID_SPAN)
                for kind, blocks in enumerate((branch, lse)):
                    base = (2 * s + kind) * groups
                    picked[t, base : base + groups] = pick(blocks, bits)
        tiles = range(part * PART_TILES, (part + 1) * PART_TILES)
        pairs = [(own.at[0, t], state_out.at[t]) for t in tiles]
        pairs += [(picked.at[t], state_out.at[D // TILE + t, : 2 * wide * groups]) for t in tiles]
        leaving += flights(pairs, out_sems.at[part])
    for copy in leaving:
        copy.wait()


def owned_kernel(wide, recv_ref, back_out, back, out_sems):
    groups = recv_ref.shape[0] // (3 * MID_SPAN)
    head = lax.rem(lax.axis_index("seq"), H)
    lane = lax.broadcasted_iota(jnp.int32, (1, TILE), 1)
    row_place = (lane - head * HD) & (TILE - 1)

    def rows_of(x):
        starts = [(3 * peer + x) * groups for peer in range(MID_SPAN)]
        return jnp.concatenate([recv_ref[start : start + groups, :] for start in starts], axis=0)

    q, k, v = (rows_of(x) for x in range(3))
    full_lane = lax.broadcasted_iota(jnp.int32, (q.shape[0], TILE), 1)
    place = (full_lane - head * HD) & (TILE - 1)
    num_den = None
    tops = jnp.zeros((q.shape[0], TILE), F32)
    for s in range(wide):
        low = scale_lane(s)
        columns = inside(row_place, low, low + HD)
        totals = columns + inside(row_place, STAT_LANE[s], STAT_LANE[s] + 3)
        scores = lax.dot_general(q * columns, k, (((1,), (1,)), ((), ())), preferred_element_type=F32)
        probs, top = probabilities(scores)
        weights = jnp.concatenate([v * columns, jnp.broadcast_to(totals, v.shape)], axis=1)
        result = jnp.dot(probs, weights, preferred_element_type=F32)
        num_den = result if num_den is None else num_den + result
        tops = jnp.where((place >= STAT_LANE[s]) & (place < STAT_LANE[s] + 3), top, tops)
    den = num_den[:, TILE:]
    used = den > F32(0.0)
    den = jnp.where(used, den, F32(1.0))
    branch = num_den[:, :TILE] / den
    lse = tops * F32(SCALE) + jnp.log(den)
    first = lse.astype(BF).astype(F32)
    second = (lse - first).astype(BF).astype(F32)
    third = lse - first - second
    stat = place
    for s in range(wide):
        stat = jnp.where(place >= STAT_LANE[s], place - STAT_LANE[s], stat)
    split = jnp.where(stat == 0, first, jnp.where(stat == 1, second, third))
    split = jnp.where(used, split, F32(0.0))
    back[...] = jnp.where(place < wide * HD, branch, split).astype(BF)
    for copy in flights([(back, back_out)], out_sems):
        copy.wait()


def merge_kernel(wide, offsets_ref, back_ref, state_ref, out_ref, base, picked, out, in_sems, out_sems):
    rows = out_ref.shape[0]
    groups = rows // MID_SPAN
    arrivals = []
    for part in range(PARTS):
        tiles = range(part * PART_TILES, (part + 1) * PART_TILES)
        pairs = [(state_ref.at[D // TILE + t, : 2 * wide * groups], picked.at[t]) for t in tiles]
        pairs += [(state_ref.at[t], base.at[t]) for t in tiles]
        arrivals.append(flights(pairs, in_sems.at[part]))
    lane = lax.broadcasted_iota(jnp.int32, (1, TILE), 1)
    full_lane = lax.broadcasted_iota(jnp.int32, (groups, TILE), 1)
    ones = jnp.ones((TILE, TILE), BF)
    branches, lses = [], []
    for s in range(wide):
        turned, stats = [], []
        for h in range(H):
            mine = back_ref[h * groups : (h + 1) * groups, :]
            place = (lane - h * HD) & (TILE - 1)
            stats.append(mine * inside(place, STAT_LANE[s], STAT_LANE[s] + 3))
            single = mine.astype(F32)
            turned.append(pltpu.roll(single, TILE - scale_lane(s), 1) if s else single)
        branches.append(turned)
        lses.append(jnp.dot(jnp.concatenate(stats, axis=0), ones, preferred_element_type=F32))

    def by_tile(t, of_head):
        heads = list(heads_of(t))
        result = of_head(heads[0])
        for h in heads[1:]:
            result = jnp.where(full_lane >= h * HD - t * TILE, of_head(h), result)
        return result

    leaving = []
    for part in range(PARTS):
        here = lanes_of(part)
        for copy in arrivals[part]:
            copy.wait()
        for t in range(part * PART_TILES, (part + 1) * PART_TILES):
            offs, results = [], []
            for s in range(wide):
                start = 2 * s * groups
                branch, lse = picked[t, start : start + groups], picked[t, start + groups : start + 2 * groups]
                offs.append(tile_offsets(offsets_ref, 1 + s, t, groups))
                for before, (other_branch, other_lse) in zip(offs, results):
                    branch = jnp.where(before == offs[s], other_branch, branch)
                    lse = jnp.where(before == offs[s], other_lse, lse)
                wide_branch = by_tile(t, lambda h: branches[s][h])
                wide_lse = by_tile(t, lambda h: lses[s][h * groups : (h + 1) * groups])
                results.append(combine(branch, lse, wide_branch, wide_lse))
            for o in range(MID_SPAN):
                block = base[t, every(o, rows), :]
                for off, (branch, _) in zip(offs, results):
                    block = jnp.where(off == o, branch, block)
                base[t, every(o, rows), :] = block
            out[:, t * TILE : (t + 1) * TILE] = base[t].astype(BF)
        leaving += flights([(out.at[:, here], out_ref.at[:, here])], out_sems.at[part])
    for copy in leaving:
        copy.wait()


def far_by_gather(queries, key_rows, value_rows, choose, dilation):
    rows = queries.shape[0]

    def select(data):
        shaped = data.reshape(rows // dilation, dilation, H, HD)
        return jnp.take_along_axis(shaped, choose[None, None, :, None], axis=1)[:, 0]

    def gathered(data):
        flat = lax.all_gather(select(data).reshape(-1, D), "seq", axis=0, tiled=True)
        return flat.reshape(-1, H, HD)

    keys, values = gathered(key_rows), gathered(value_rows)
    scores = jnp.einsum("qhd,khd->hqk", select(queries), keys, preferred_element_type=F32) * SCALE
    top = jnp.max(scores, axis=-1, keepdims=True)
    expo = jnp.exp(scores - top)
    total = jnp.sum(expo, axis=-1)
    mixed = jnp.einsum("hqk,khd->qhd", expo.astype(BF), values, preferred_element_type=F32)
    mixed = mixed / jnp.transpose(total)[:, :, None]
    lse = jnp.transpose(top[..., 0] + jnp.log(total))
    selected = jnp.arange(dilation)[:, None] == choose[None, :]
    full_mixed = jnp.where(selected[None, :, :, None], mixed[:, None], F32(0.0)).reshape(rows, D)
    full_lse = jnp.where(selected[None], lse[:, None], F32(-1e30)).reshape(rows, H)
    full_lse = jnp.repeat(full_lse, HD, axis=1)

    def tiled(data):
        return data.reshape(rows, D // TILE, TILE).swapaxes(0, 1)

    return tiled(full_mixed), tiled(full_lse)


def exchange(blocks):
    count = lax.axis_size("seq")
    teams = None
    if count != MID_SPAN:
        teams = [[first + i for i in range(MID_SPAN)] for first in range(0, count, MID_SPAN)]
    return lax.all_to_all(blocks, "seq", 0, 0, axis_index_groups=teams, tiled=True)


def shards(queries, key_rows, value_rows, offsets):
    rows = queries.shape[0]
    count = lax.axis_size("seq")
    wide = 2 if count == MID_SPAN else 1
    groups = rows // MID_SPAN
    near_rows = rows // NEAR_SPAN
    send_rows = H * 3 * groups
    back_rows = H * groups
    smem = pl.BlockSpec(memory_space=pltpu.SMEM)
    vmem = pl.BlockSpec(memory_space=pltpu.VMEM)
    hbm = pl.BlockSpec(memory_space=pltpu.HBM)
    shape = jax.ShapeDtypeStruct

    def sems(*count):
        return pltpu.SemaphoreType.DMA(count)

    near_q, near_kv, send = pl.pallas_call(
        functools.partial(prep_kernel, wide),
        out_shape=(
            shape((near_rows, D), BF),
            shape((2 * near_rows, D), BF),
            shape((send_rows, TILE), BF),
        ),
        in_specs=[smem, hbm, hbm, hbm],
        out_specs=(hbm, hbm, hbm),
        scratch_shapes=[
            pltpu.VMEM((3, rows, D), BF),
            pltpu.VMEM((3, D // TILE, rows, TILE), F32),
            pltpu.VMEM((near_rows, D), BF),
            pltpu.VMEM((2 * near_rows, D), BF),
            pltpu.VMEM((send_rows, TILE), BF),
            sems(PARTS * 3),
            sems(PARTS, 3),
        ],
        compiler_params=params(),
        cost_estimate=cost(6 * rows * D, 10 * rows * D),
        name="prep",
    )(offsets, queries, key_rows, value_rows)

    near_side = from_partner(near_kv, "seq", 2)
    near_core = from_partner(near_kv, "seq", 1)
    recv = exchange(send)

    tiled = (2, D // TILE, rows, TILE)
    own = pl.pallas_call(
        local_kernel,
        out_shape=shape(tiled, F32),
        in_specs=[hbm] * 3,
        out_specs=hbm,
        scratch_shapes=[pltpu.VMEM((3, rows, D), BF), pltpu.VMEM(tiled, F32), sems(PARTS * 3), sems(PARTS, 2 * PART_TILES)],
        compiler_params=params(),
        cost_estimate=cost(400 * rows * rows * H * 256, 14 * rows * D, rows * rows * H),
        name="local",
    )(queries, key_rows, value_rows)
    own, recv, near_side = lax.optimization_barrier((own, recv, near_side))

    near_both = from_partner(near_side, "seq", 1)
    back = pl.pallas_call(
        functools.partial(owned_kernel, wide),
        out_shape=shape((back_rows, TILE), BF),
        in_specs=[vmem],
        out_specs=hbm,
        scratch_shapes=[pltpu.VMEM((back_rows, TILE), BF), sems(1)],
        compiler_params=params(OWNED_BYTES),
        cost_estimate=cost(4 * wide * rows * rows * 256, 2 * send_rows * TILE, wide * rows * rows),
        name="owned",
    )(recv)
    back = exchange(back)

    if wide == 1:
        far_branch, far_lse = far_by_gather(queries, key_rows, value_rows, offsets[2], count)
        own = jnp.stack(combine(own[0], own[1], far_branch, far_lse))
    state = pl.pallas_call(
        functools.partial(near_kernel, wide),
        out_shape=shape((12 * D // TILE, rows, TILE), F32),
        in_specs=[smem] + [hbm] * (2 + NEAR_SPAN),
        out_specs=hbm,
        scratch_shapes=[
            pltpu.VMEM((near_rows, D), BF),
            pltpu.VMEM((2, NEAR_SPAN * near_rows, D), BF),
            pltpu.VMEM(tiled, F32),
            pltpu.VMEM((D // TILE, 2 * wide * groups, TILE), F32),
            sems(PARTS, 1 + 2 * NEAR_SPAN),
            sems(PARTS, 2 * PART_TILES),
            sems(PARTS, 2 * PART_TILES),
        ],
        compiler_params=params(),
        cost_estimate=cost(4 * near_rows * rows * H * 256, 8 * rows * D, near_rows * rows * H),
        name="near",
    )(offsets, near_q, near_kv, near_core, near_side, near_both, own)
    state, back = lax.optimization_barrier((state, back))

    return pl.pallas_call(
        functools.partial(merge_kernel, wide),
        out_shape=shape((rows, D), BF),
        in_specs=[smem, vmem, hbm],
        out_specs=hbm,
        scratch_shapes=[
            pltpu.VMEM((D // TILE, rows, TILE), F32),
            pltpu.VMEM((D // TILE, 2 * wide * groups, TILE), F32),
            pltpu.VMEM((rows, D), BF),
            sems(PARTS, 2 * PART_TILES),
            sems(PARTS, 1),
        ],
        compiler_params=params(SMALL_BYTES),
        cost_estimate=cost(2 * rows * rows * D, 14 * rows * D),
        name="merge",
    )(offsets, back, state)


def solution(mesh):
    in_specs = (
        P(("slides", "seq"), None),
        P(("slides", "seq"), None),
        P(("slides", "seq"), None),
        P(),
    )
    out_specs = P(("slides", "seq"), None)
    return jax.shard_map(shards, mesh=mesh, in_specs=in_specs, out_specs=out_specs, check_vma=False)
```

```python
import functools

import jax
import jax.numpy as jnp
from jax import lax
from jax.experimental import pallas as pl
from jax.experimental.pallas import tpu as pltpu
from jax.sharding import PartitionSpec as P

H = 16
HD = 48
D = 768
NEAR_SPAN = 4
MID_SPAN = 16
HALF = 384
TILE = 128
HALF_HEADS = HALF // HD
PARTS = D // HALF
PART_TILES = HALF // TILE
STAT_LANE = (2 * HD, 2 * HD + 16)
SPARE = TILE - 2 * HD
SECTION = 256
PITCH = 36
SCALE = HD ** (-0.5)
LOG2E = 1.4426950408889634
VMEM_BYTES = 63 * 1024 * 1024
SMALL_BYTES = 48 * 1024 * 1024
OWNED_BYTES = 32 * 1024 * 1024
BF = jnp.bfloat16
F32 = jnp.float32


def from_partner(block, axis, flip):
    count = lax.axis_size(axis)
    return lax.ppermute(block, axis, [(i, i ^ flip) for i in range(count)])


def params(limit=VMEM_BYTES):
    return pltpu.CompilerParams(vmem_limit_bytes=limit)


def cost(flops, moved, exps=0):
    return pl.CostEstimate(flops=flops, bytes_accessed=moved, transcendentals=exps)


def tile_offsets(offsets_ref, scale, tile, rows):
    lane = lax.broadcasted_iota(jnp.int32, (rows, TILE), 1)
    heads = list(heads_of(tile))
    result = jnp.full((rows, TILE), offsets_ref[scale, heads[0]], jnp.int32)
    for h in heads[1:]:
        result = jnp.where(lane >= h * HD - tile * TILE, offsets_ref[scale, h], result)
    return result


def inside(lane, low, high):
    return jnp.where((lane >= low) & (lane < high), F32(1.0), F32(0.0)).astype(BF)


def heads_of(tile):
    return range(tile * TILE // HD, ((tile + 1) * TILE - 1) // HD + 1)


def tiles_of(head):
    return range(head * HD // TILE, ((head + 1) * HD - 1) // TILE + 1)


def every(first, chunk):
    return pl.ds(first + MID_SPAN * 8 * chunk, 8, stride=MID_SPAN)


def bits_of(offs, count):
    return [(offs & (1 << k)) != 0 for k in range(count.bit_length() - 1)]


def pick(blocks, bits):
    for bit in bits:
        blocks = [jnp.where(bit, high, low) for low, high in zip(blocks[::2], blocks[1::2])]
    return blocks[0]


def tile_lanes(tile):
    return slice(tile * TILE, (tile + 1) * TILE)


def lanes_of(part):
    return slice(part * HALF, (part + 1) * HALF)


def flights(pairs, sems):
    copies = [pltpu.make_async_copy(src, dst, sems.at[i]) for i, (src, dst) in enumerate(pairs)]
    for copy in copies:
        copy.start()
    return copies


def scale_lane(scale):
    return scale * HD


def spare_turn(piece):
    return (2 * HD - piece * SPARE) % TILE


def folded(place, chunks):
    result = []
    for first in range(0, len(chunks), 4):
        last = chunks[first + 3]
        for piece in range(3):
            moved = pltpu.roll(last, spare_turn(piece), 1) if spare_turn(piece) else last
            result.append(jnp.where(place < 2 * HD, chunks[first + piece], moved))
    return result


def unfolded(place, chunks):
    result = []
    for first in range(0, len(chunks), 3):
        last = None
        for piece in range(3):
            turn = (TILE - spare_turn(piece)) % TILE
            moved = pltpu.roll(chunks[first + piece], turn, 1) if turn else chunks[first + piece]
            last = moved if last is None else jnp.where(place >= piece * SPARE, moved, last)
        result += chunks[first : first + 3] + [last]
    return result


def prep_kernel(
    wide, offsets_ref, q_ref, k_ref, v_ref, near_q_out, near_out, send_out,
    stage, single, near_q, near, send, in_sems, out_sems,
):
    rows = q_ref.shape[0]
    groups = rows // MID_SPAN
    near_rows = rows // NEAR_SPAN
    tiles = range(D // TILE)
    sections = [slice(c * SECTION, (c + 1) * SECTION) for c in range(rows // SECTION)]
    arrivals = [
        flights([(ref.at[section], stage.at[x, section]) for x, ref in enumerate((q_ref, k_ref, v_ref))], in_sems.at[c])
        for c, section in enumerate(sections)
    ]
    lane = lax.broadcasted_iota(jnp.int32, (8, TILE), 1)
    near_bits = [bits_of(tile_offsets(offsets_ref, 0, t, 8), NEAR_SPAN) for t in tiles]
    wide_bits = [[bits_of(tile_offsets(offsets_ref, 1 + s, t, 8), MID_SPAN) for t in tiles] for s in range(wide)]
    chosen = {}
    for c, section in enumerate(sections):
        kept = SECTION // MID_SPAN
        for x in range(3):
            arrivals[c][x].wait()
            for t in tiles:
                lanes = tile_lanes(t)
                spread = stage[x, section, lanes].astype(F32)
                for g in range(kept):
                    for i in range(2):
                        at = g * MID_SPAN + 8 * i
                        single[x, t, pl.ds(c * kept + g + 8 * i * PITCH, 8, stride=PITCH), :] = spread[at : at + 8]
                near_parts = [[] for _ in range(NEAR_SPAN)]
                for chunk in range(c * kept // 8, (c + 1) * kept // 8):
                    block = [single[x, t, o * PITCH + 8 * chunk : o * PITCH + 8 * chunk + 8, :] for o in range(MID_SPAN)]
                    for a in range(NEAR_SPAN):
                        near_parts[a].append(pick(block[a * NEAR_SPAN : (a + 1) * NEAR_SPAN], near_bits[t]))
                    for s in range(wide):
                        picked = pick(block, wide_bits[s][t])
                        chosen[x, s, t, chunk] = pltpu.roll(picked, scale_lane(s), 1) if s else picked
                for a in range(NEAR_SPAN):
                    near_block = jnp.concatenate(near_parts[a], axis=0).astype(BF)
                    base = a * groups + c * kept
                    if x == 0:
                        near_q[base : base + kept, lanes] = near_block
                    else:
                        base += (x - 1) * near_rows
                        near[base : base + kept, lanes] = near_block
    leaving = flights([(near, near_out), (near_q, near_q_out)], out_sems.at[0])
    for h in range(H):
        travel = []
        for x in range(3):
            chunks = []
            for chunk in range(groups // 8):
                joined = jnp.zeros((8, TILE), F32)
                for s in range(wide):
                    for t in tiles_of(h):
                        low, high = max(h * HD, t * TILE), min((h + 1) * HD, (t + 1) * TILE)
                        turned = (lane - scale_lane(s)) & (TILE - 1)
                        hit = (turned >= low - t * TILE) & (turned < high - t * TILE)
                        joined = jnp.where(hit, chosen[x, s, t, chunk], joined)
                chunks.append(joined)
            travel += folded((lane - h * HD) & (TILE - 1), chunks)
        send[h] = jnp.concatenate(travel, axis=0).astype(BF)
        if h == H // 2 - 1:
            leaving += flights([(send.at[: H // 2], send_out.at[: H // 2])], out_sems.at[1])
    leaving += flights([(send.at[H // 2 :], send_out.at[H // 2 :])], out_sems.at[2])
    for copy in leaving:
        copy.wait()


def probabilities(scores):
    top = jnp.max(scores, axis=1, keepdims=True)
    return jnp.exp2((scores - top) * F32(SCALE * LOG2E)).astype(BF), top


def attend_half(q, k, v, stacked):
    count = q.shape[0]
    lane = lax.broadcasted_iota(jnp.int32, (1, TILE), 1)
    full_lane = lax.broadcasted_iota(jnp.int32, (count, TILE), 1)
    wide_lane = lax.broadcasted_iota(jnp.int32, (1, 2 * TILE), 1)
    num = [None] * 3
    den = [None] * 3
    top_tiles = [jnp.zeros((count, TILE), F32) for _ in range(3)]

    def add(into, tile, value):
        into[tile] = value if into[tile] is None else into[tile] + value

    def masked_query(h, start):
        return q[:, start : start + 2 * TILE] * inside(wide_lane, h * HD - start, (h + 1) * HD - start)

    def scores_of(left, start):
        right = k[:, start : start + 2 * TILE]
        return lax.dot_general(left, right, (((1,), (1,)), ((), ())), preferred_element_type=F32)

    starts = [0 if (h + 1) * HD <= 2 * TILE else TILE for h in range(HALF_HEADS)]
    ready = {}
    if stacked:
        for start in (0, TILE):
            members = [h for h in range(HALF_HEADS) if starts[h] == start]
            together = scores_of(jnp.concatenate([masked_query(h, start) for h in members], axis=0), start)
            for i, h in enumerate(members):
                ready[h] = together[i * count : (i + 1) * count]
    for h in range(HALF_HEADS):
        low, high = h * HD, (h + 1) * HD
        scores = ready[h] if stacked else scores_of(masked_query(h, starts[h]), starts[h])
        probs, top = probabilities(scores)
        first, last = low // TILE, (high - 1) // TILE
        inside_first = (full_lane >= low - first * TILE) & (full_lane < high - first * TILE)
        ones_first = inside(lane, low - first * TILE, high - first * TILE)
        v_first = v[:, first * TILE : (first + 1) * TILE] * ones_first
        if first == last:
            weights = jnp.concatenate([v_first, jnp.broadcast_to(ones_first, v_first.shape)], axis=1)
            result = jnp.dot(probs, weights, preferred_element_type=F32)
            add(num, first, result[:, :TILE])
            add(den, first, result[:, TILE:])
            top_tiles[first] = jnp.where(inside_first, top, top_tiles[first])
        else:
            inside_last = full_lane < high - last * TILE
            ones_last = inside(lane, 0, high - last * TILE)
            v_last = v[:, last * TILE : (last + 1) * TILE] * ones_last
            weights = jnp.concatenate([v_first + ones_last, v_last + ones_first], axis=1)
            result = jnp.dot(probs, weights, preferred_element_type=F32)
            left, right = result[:, :TILE], result[:, TILE:]
            zero = F32(0.0)
            add(num, first, jnp.where(inside_first, left, zero))
            add(den, first, jnp.where(inside_first, right, zero))
            add(num, last, jnp.where(inside_last, right, zero))
            add(den, last, jnp.where(inside_last, left, zero))
            top_tiles[first] = jnp.where(inside_first, top, top_tiles[first])
            top_tiles[last] = jnp.where(inside_last, top, top_tiles[last])
    branch = [n / d for n, d in zip(num, den)]
    lse = [t * F32(SCALE) + jnp.log(d) for t, d in zip(top_tiles, den)]
    return branch, lse


def local_kernel(q_ref, k_ref, v_ref, own_out, stage, own, in_sems, out_sems):
    arrivals = flights(
        [
            (ref.at[:, lanes_of(part)], stage.at[x, :, lanes_of(part)])
            for part in range(PARTS)
            for x, ref in enumerate((q_ref, k_ref, v_ref))
        ],
        in_sems,
    )
    leaving = []
    for part in range(PARTS):
        here = lanes_of(part)
        for x in range(3):
            arrivals[part * 3 + x].wait()
        branch_tiles, lse_tiles = attend_half(stage[0, :, here], stage[1, :, here], stage[2, :, here], False)
        for t in range(PART_TILES):
            own[0, part * PART_TILES + t] = branch_tiles[t]
            own[1, part * PART_TILES + t] = lse_tiles[t]
        tiles = range(part * PART_TILES, (part + 1) * PART_TILES)
        leaving += flights([(own.at[i, t], own_out.at[i, t]) for i in range(2) for t in tiles], out_sems.at[part])
    for copy in leaving:
        copy.wait()


def combine(branch_a, lse_a, branch_b, lse_b):
    high = jnp.maximum(lse_a, lse_b)
    weight_a = jnp.exp(lse_a - high)
    weight_b = jnp.exp(lse_b - high)
    total = weight_a + weight_b
    return (weight_a * branch_a + weight_b * branch_b) / total, high + jnp.log(total)


def near_kernel(wide, offsets_ref, q_ref, *refs):
    kv_refs, (own_ref, state_out) = refs[:NEAR_SPAN], refs[NEAR_SPAN : NEAR_SPAN + 2]
    q_stage, kv_stage, own, picked, kv_sems, own_sems, out_sems = refs[NEAR_SPAN + 2 :]
    near_rows = q_ref.shape[0]
    rows = own_ref.shape[2]
    groups = rows // MID_SPAN
    arrivals, own_arrivals, leaving = [], [], []
    for part in range(PARTS):
        here = lanes_of(part)
        pairs = [(q_ref.at[:, here], q_stage.at[:, here])]
        for i, ref in enumerate(kv_refs):
            for x in range(2):
                rows_x = slice(x * near_rows, (x + 1) * near_rows)
                rows_i = slice(i * near_rows, (i + 1) * near_rows)
                pairs.append((ref.at[rows_x, here], kv_stage.at[x, rows_i, here]))
        arrivals.append(flights(pairs, kv_sems.at[part]))
        tiles = range(part * PART_TILES, (part + 1) * PART_TILES)
        own_arrivals.append(
            flights([(own_ref.at[i, t], own.at[i, t]) for i in range(2) for t in tiles], own_sems.at[part])
        )
    for part in range(PARTS):
        here = lanes_of(part)
        for copy in arrivals[part]:
            copy.wait()
        near_branch, near_lse = attend_half(q_stage[:, here], kv_stage[0, :, here], kv_stage[1, :, here], True)
        for copy in own_arrivals[part]:
            copy.wait()
        for i in range(PART_TILES):
            t = part * PART_TILES + i
            offs = tile_offsets(offsets_ref, 0, t, 8)
            hits, bits = [offs == b for b in range(NEAR_SPAN)], bits_of(offs, NEAR_SPAN)
            wide_bits = [bits_of(tile_offsets(offsets_ref, 1 + s, t, 8), MID_SPAN) for s in range(wide)]
            for chunk in range(groups // 8):
                branch = [own[0, t, every(o, chunk), :] for o in range(MID_SPAN)]
                lse = [own[1, t, every(o, chunk), :] for o in range(MID_SPAN)]
                for a in range(NEAR_SPAN):
                    members = slice(a * NEAR_SPAN, (a + 1) * NEAR_SPAN)
                    span = slice(a * groups + chunk * 8, a * groups + (chunk + 1) * 8)
                    mixed, high = combine(
                        pick(branch[members], bits), pick(lse[members], bits), near_branch[i][span], near_lse[i][span]
                    )
                    for b, hit in enumerate(hits):
                        o = a * NEAR_SPAN + b
                        branch[o] = jnp.where(hit, mixed, branch[o])
                        lse[o] = jnp.where(hit, high, lse[o])
                        own[0, t, every(o, chunk), :] = branch[o]
                for s in range(wide):
                    for kind, blocks in enumerate((branch, lse)):
                        base = (2 * s + kind) * groups + chunk * 8
                        picked[t, base : base + 8] = pick(blocks, wide_bits[s])
        tiles = range(part * PART_TILES, (part + 1) * PART_TILES)
        pairs = [(own.at[0, t], state_out.at[t]) for t in tiles]
        pairs += [(picked.at[t], state_out.at[D // TILE + t, : 2 * wide * groups]) for t in tiles]
        leaving += flights(pairs, out_sems.at[part])
    for copy in leaving:
        copy.wait()


def owned_kernel(wide, recv_ref, back_out, back, out_sems):
    third = recv_ref.shape[1] // 3
    groups = third * 4 // 3
    head = lax.rem(lax.axis_index("seq"), H)
    lane = lax.broadcasted_iota(jnp.int32, (1, TILE), 1)
    row_place = (lane - head * HD) & (TILE - 1)
    chunk_place = (lax.broadcasted_iota(jnp.int32, (8, TILE), 1) - head * HD) & (TILE - 1)
    peers = [recv_ref[peer].astype(F32) for peer in range(MID_SPAN)]

    def rows_of(x):
        found = []
        for peer in peers:
            chunks = [peer[r : r + 8] for r in range(x * third, (x + 1) * third, 8)]
            found += unfolded(chunk_place, chunks)
        return jnp.concatenate(found, axis=0).astype(BF)

    q, k, v = (rows_of(x) for x in range(3))
    full_lane = lax.broadcasted_iota(jnp.int32, (q.shape[0], TILE), 1)
    place = (full_lane - head * HD) & (TILE - 1)
    num_den = None
    tops = jnp.zeros((q.shape[0], TILE), F32)
    for s in range(wide):
        low = scale_lane(s)
        columns = inside(row_place, low, low + HD)
        totals = columns + inside(row_place, STAT_LANE[s], STAT_LANE[s] + 3)
        scores = lax.dot_general(q * columns, k, (((1,), (1,)), ((), ())), preferred_element_type=F32)
        probs, top = probabilities(scores)
        weights = jnp.concatenate([v * columns, jnp.broadcast_to(totals, v.shape)], axis=1)
        result = jnp.dot(probs, weights, preferred_element_type=F32)
        num_den = result if num_den is None else num_den + result
        tops = jnp.where((place >= STAT_LANE[s]) & (place < STAT_LANE[s] + 3), top, tops)
    den = num_den[:, TILE:]
    used = den > F32(0.0)
    den = jnp.where(used, den, F32(1.0))
    branch = num_den[:, :TILE] / den
    lse = tops * F32(SCALE) + jnp.log(den)
    first = lse.astype(BF).astype(F32)
    second = (lse - first).astype(BF).astype(F32)
    third = lse - first - second
    stat = place
    for s in range(wide):
        stat = jnp.where(place >= STAT_LANE[s], place - STAT_LANE[s], stat)
    split = jnp.where(stat == 0, first, jnp.where(stat == 1, second, third))
    split = jnp.where(used, split, F32(0.0))
    back[...] = jnp.where(place < wide * HD, branch, split).astype(BF)
    for copy in flights([(back, back_out)], out_sems):
        copy.wait()


def merge_kernel(wide, offsets_ref, back_ref, state_ref, out_ref, base, picked, out, in_sems, out_sems):
    rows = out_ref.shape[0]
    groups = rows // MID_SPAN
    arrivals = [
        flights(
            [(state_ref.at[D // TILE + t, : 2 * wide * groups], picked.at[t]), (state_ref.at[t], base.at[t])], in_sems.at[t]
        )
        for t in range(D // TILE)
    ]
    lane = lax.broadcasted_iota(jnp.int32, (1, TILE), 1)
    full_lane = lax.broadcasted_iota(jnp.int32, (groups, TILE), 1)
    row_in_16 = lax.broadcasted_iota(jnp.int32, (MID_SPAN, TILE), 0)
    ones = jnp.ones((TILE, TILE), BF)
    branches, lses = [], []
    for s in range(wide):
        turned, stats = [], []
        for h in range(H):
            mine = back_ref[h * groups : (h + 1) * groups, :]
            place = (lane - h * HD) & (TILE - 1)
            stats.append(mine * inside(place, STAT_LANE[s], STAT_LANE[s] + 3))
            single = mine.astype(F32)
            turned.append(pltpu.roll(single, TILE - scale_lane(s), 1) if s else single)
        branches.append(turned)
        lses.append(jnp.dot(jnp.concatenate(stats, axis=0), ones, preferred_element_type=F32))

    def by_tile(t, of_head):
        heads = list(heads_of(t))
        result = of_head(heads[0])
        for h in heads[1:]:
            result = jnp.where(full_lane >= h * HD - t * TILE, of_head(h), result)
        return result

    leaving = []
    for t in range(D // TILE):
        lanes = tile_lanes(t)
        arrivals[t][0].wait()
        offs, results = [], []
        for s in range(wide):
            start = 2 * s * groups
            branch, lse = picked[t, start : start + groups], picked[t, start + groups : start + 2 * groups]
            offs.append(tile_offsets(offsets_ref, 1 + s, t, MID_SPAN))
            for before, (other_branch, other_lse) in zip(offs, results):
                same = jnp.concatenate([before - offs[s]] * (groups // MID_SPAN), axis=0) == 0
                branch = jnp.where(same, other_branch, branch)
                lse = jnp.where(same, other_lse, lse)
            wide_branch = by_tile(t, lambda h: branches[s][h])
            wide_lse = by_tile(t, lambda h: lses[s][h * groups : (h + 1) * groups])
            results.append(combine(branch, lse, wide_branch, wide_lse))
        hits = [row_in_16 == off for off in offs]
        arrivals[t][1].wait()
        for g in range(groups):
            block = base[t, g * MID_SPAN : (g + 1) * MID_SPAN]
            for hit, (branch, _) in zip(hits, results):
                block = jnp.where(hit, jnp.broadcast_to(branch[g : g + 1], (MID_SPAN, TILE)), block)
            out[g * MID_SPAN : (g + 1) * MID_SPAN, lanes] = block.astype(BF)
        leaving += flights([(out.at[:, lanes], out_ref.at[:, lanes])], out_sems.at[t])
    for copy in leaving:
        copy.wait()


def far_by_gather(queries, key_rows, value_rows, choose, dilation):
    rows = queries.shape[0]

    def select(data):
        shaped = data.reshape(rows // dilation, dilation, H, HD)
        return jnp.take_along_axis(shaped, choose[None, None, :, None], axis=1)[:, 0]

    def gathered(data):
        flat = lax.all_gather(select(data).reshape(-1, D), "seq", axis=0, tiled=True)
        return flat.reshape(-1, H, HD)

    keys, values = gathered(key_rows), gathered(value_rows)
    scores = jnp.einsum("qhd,khd->hqk", select(queries), keys, preferred_element_type=F32) * SCALE
    top = jnp.max(scores, axis=-1, keepdims=True)
    expo = jnp.exp(scores - top)
    total = jnp.sum(expo, axis=-1)
    mixed = jnp.einsum("hqk,khd->qhd", expo.astype(BF), values, preferred_element_type=F32)
    mixed = mixed / jnp.transpose(total)[:, :, None]
    lse = jnp.transpose(top[..., 0] + jnp.log(total))
    selected = jnp.arange(dilation)[:, None] == choose[None, :]
    full_mixed = jnp.where(selected[None, :, :, None], mixed[:, None], F32(0.0)).reshape(rows, D)
    full_lse = jnp.where(selected[None], lse[:, None], F32(-1e30)).reshape(rows, H)
    full_lse = jnp.repeat(full_lse, HD, axis=1)

    def tiled(data):
        return data.reshape(rows, D // TILE, TILE).swapaxes(0, 1)

    return tiled(full_mixed), tiled(full_lse)


def exchange(blocks):
    count = lax.axis_size("seq")
    teams = None
    if count != MID_SPAN:
        teams = [[first + i for i in range(MID_SPAN)] for first in range(0, count, MID_SPAN)]
    return lax.all_to_all(blocks, "seq", 0, 0, axis_index_groups=teams, tiled=True)


def shards(queries, key_rows, value_rows, offsets):
    rows = queries.shape[0]
    count = lax.axis_size("seq")
    wide = 2 if count == MID_SPAN else 1
    groups = rows // MID_SPAN
    near_rows = rows // NEAR_SPAN
    send_shape = (H, 3 * groups * 3 // 4, TILE)
    back_rows = H * groups
    smem = pl.BlockSpec(memory_space=pltpu.SMEM)
    vmem = pl.BlockSpec(memory_space=pltpu.VMEM)
    hbm = pl.BlockSpec(memory_space=pltpu.HBM)
    shape = jax.ShapeDtypeStruct

    def sems(*count):
        return pltpu.SemaphoreType.DMA(count)

    near_q, near_kv, send = pl.pallas_call(
        functools.partial(prep_kernel, wide),
        out_shape=(
            shape((near_rows, D), BF),
            shape((2 * near_rows, D), BF),
            shape(send_shape, BF),
        ),
        in_specs=[smem, hbm, hbm, hbm],
        out_specs=(hbm, hbm, hbm),
        scratch_shapes=[
            pltpu.VMEM((3, rows, D), BF),
            pltpu.VMEM((3, D // TILE, MID_SPAN * PITCH, TILE), F32),
            pltpu.VMEM((near_rows, D), BF),
            pltpu.VMEM((2 * near_rows, D), BF),
            pltpu.VMEM(send_shape, BF),
            sems(rows // SECTION, 3),
            sems(3, 2),
        ],
        compiler_params=params(),
        cost_estimate=cost(6 * rows * D, 10 * rows * D),
        name="prep",
    )(offsets, queries, key_rows, value_rows)

    near_side = from_partner(near_kv, "seq", 2)
    near_core = from_partner(near_kv, "seq", 1)
    recv = exchange(send)

    tiled = (2, D // TILE, rows, TILE)
    own = pl.pallas_call(
        local_kernel,
        out_shape=shape(tiled, F32),
        in_specs=[hbm] * 3,
        out_specs=hbm,
        scratch_shapes=[pltpu.VMEM((3, rows, D), BF), pltpu.VMEM(tiled, F32), sems(PARTS * 3), sems(PARTS, 2 * PART_TILES)],
        compiler_params=params(),
        cost_estimate=cost(16 * rows * rows * H * 256, 14 * rows * D, rows * rows * H),
        name="local",
    )(queries, key_rows, value_rows)
    own, recv, near_side = lax.optimization_barrier((own, recv, near_side))

    near_both = from_partner(near_side, "seq", 1)
    back = pl.pallas_call(
        functools.partial(owned_kernel, wide),
        out_shape=shape((back_rows, TILE), BF),
        in_specs=[vmem],
        out_specs=hbm,
        scratch_shapes=[pltpu.VMEM((back_rows, TILE), BF), sems(1)],
        compiler_params=params(OWNED_BYTES),
        cost_estimate=cost(4 * wide * rows * rows * 256, 4 * rows * D, wide * rows * rows),
        name="owned",
    )(recv)
    back = exchange(back)

    if wide == 1:
        far_branch, far_lse = far_by_gather(queries, key_rows, value_rows, offsets[2], count)
        own = jnp.stack(combine(own[0], own[1], far_branch, far_lse))
    state = pl.pallas_call(
        functools.partial(near_kernel, wide),
        out_shape=shape((12 * D // TILE, rows, TILE), F32),
        in_specs=[smem] + [hbm] * (2 + NEAR_SPAN),
        out_specs=hbm,
        scratch_shapes=[
            pltpu.VMEM((near_rows, D), BF),
            pltpu.VMEM((2, NEAR_SPAN * near_rows, D), BF),
            pltpu.VMEM(tiled, F32),
            pltpu.VMEM((D // TILE, 2 * wide * groups, TILE), F32),
            sems(PARTS, 1 + 2 * NEAR_SPAN),
            sems(PARTS, 2 * PART_TILES),
            sems(PARTS, 2 * PART_TILES),
        ],
        compiler_params=params(),
        cost_estimate=cost(4 * near_rows * rows * H * 256, 8 * rows * D, near_rows * rows * H),
        name="near",
    )(offsets, near_q, near_kv, near_core, near_side, near_both, own)
    state, back = lax.optimization_barrier((state, back))

    return pl.pallas_call(
        functools.partial(merge_kernel, wide),
        out_shape=shape((rows, D), BF),
        in_specs=[smem, vmem, hbm],
        out_specs=hbm,
        scratch_shapes=[
            pltpu.VMEM((D // TILE, rows, TILE), F32),
            pltpu.VMEM((D // TILE, 2 * wide * groups, TILE), F32),
            pltpu.VMEM((rows, D), BF),
            sems(D // TILE, 2),
            sems(D // TILE, 1),
        ],
        compiler_params=params(SMALL_BYTES),
        cost_estimate=cost(2 * rows * rows * D, 14 * rows * D),
        name="merge",
    )(offsets, back, state)


def solution(mesh):
    in_specs = (
        P(("slides", "seq"), None),
        P(("slides", "seq"), None),
        P(("slides", "seq"), None),
        P(),
    )
    out_specs = P(("slides", "seq"), None)
    return jax.shard_map(shards, mesh=mesh, in_specs=in_specs, out_specs=out_specs, check_vma=False)
```

```python
import functools

import jax
import jax.numpy as jnp
from jax import lax
from jax.experimental import pallas as pl
from jax.experimental.pallas import tpu as pltpu
from jax.sharding import PartitionSpec as P

H = 16
HD = 48
D = 768
NEAR_SPAN = 4
MID_SPAN = 16
HALF = 384
TILE = 128
HALF_HEADS = HALF // HD
PARTS = D // HALF
PART_TILES = HALF // TILE
STAT_LANE = (2 * HD, 2 * HD + 16)
SPARE = TILE - 2 * HD
SECTION = 256
PITCH = 36
SCALE = HD ** (-0.5)
LOG2E = 1.4426950408889634
VMEM_BYTES = 63 * 1024 * 1024
SMALL_BYTES = 48 * 1024 * 1024
OWNED_BYTES = 32 * 1024 * 1024
BF = jnp.bfloat16
F32 = jnp.float32


def from_partner(block, axis, flip):
    count = lax.axis_size(axis)
    return lax.ppermute(block, axis, [(i, i ^ flip) for i in range(count)])


def params(limit=VMEM_BYTES):
    return pltpu.CompilerParams(vmem_limit_bytes=limit)


def cost(flops, moved, exps=0):
    return pl.CostEstimate(flops=flops, bytes_accessed=moved, transcendentals=exps)


def tile_offsets(offsets_ref, scale, tile, rows):
    lane = lax.broadcasted_iota(jnp.int32, (rows, TILE), 1)
    heads = list(heads_of(tile))
    result = jnp.full((rows, TILE), offsets_ref[scale, heads[0]], jnp.int32)
    for h in heads[1:]:
        result = jnp.where(lane >= h * HD - tile * TILE, offsets_ref[scale, h], result)
    return result


def inside(lane, low, high):
    return jnp.where((lane >= low) & (lane < high), F32(1.0), F32(0.0)).astype(BF)


def heads_of(tile):
    return range(tile * TILE // HD, ((tile + 1) * TILE - 1) // HD + 1)


def tiles_of(head):
    return range(head * HD // TILE, ((head + 1) * HD - 1) // TILE + 1)


def every(first, chunk):
    return pl.ds(first + MID_SPAN * 8 * chunk, 8, stride=MID_SPAN)


def bits_of(offs, count):
    return [(offs & (1 << k)) != 0 for k in range(count.bit_length() - 1)]


def pick(blocks, bits):
    for bit in bits:
        blocks = [jnp.where(bit, high, low) for low, high in zip(blocks[::2], blocks[1::2])]
    return blocks[0]


def tile_lanes(tile):
    return slice(tile * TILE, (tile + 1) * TILE)


def lanes_of(part):
    return slice(part * HALF, (part + 1) * HALF)


def flights(pairs, sems):
    copies = [pltpu.make_async_copy(src, dst, sems.at[i]) for i, (src, dst) in enumerate(pairs)]
    for copy in copies:
        copy.start()
    return copies


def scale_lane(scale):
    return scale * HD


def spare_turn(piece):
    return (2 * HD - piece * SPARE) % TILE


def folded(place, chunks):
    result = []
    for first in range(0, len(chunks), 4):
        last = chunks[first + 3]
        for piece in range(3):
            moved = pltpu.roll(last, spare_turn(piece), 1) if spare_turn(piece) else last
            result.append(jnp.where(place < 2 * HD, chunks[first + piece], moved))
    return result


def unfolded(place, chunks):
    result = []
    for first in range(0, len(chunks), 3):
        last = None
        for piece in range(3):
            turn = (TILE - spare_turn(piece)) % TILE
            moved = pltpu.roll(chunks[first + piece], turn, 1) if turn else chunks[first + piece]
            last = moved if last is None else jnp.where(place >= piece * SPARE, moved, last)
        result += chunks[first : first + 3] + [last]
    return result


def prep_kernel(
    wide, offsets_ref, q_ref, k_ref, v_ref, near_q_out, near_out, send_out,
    stage, single, near_q, near, send, in_sems, out_sems,
):
    rows = q_ref.shape[0]
    groups = rows // MID_SPAN
    near_rows = rows // NEAR_SPAN
    tiles = range(D // TILE)
    sections = [slice(c * SECTION, (c + 1) * SECTION) for c in range(rows // SECTION)]
    arrivals = [
        flights([(ref.at[section], stage.at[x, section]) for x, ref in enumerate((q_ref, k_ref, v_ref))], in_sems.at[c])
        for c, section in enumerate(sections)
    ]
    lane = lax.broadcasted_iota(jnp.int32, (8, TILE), 1)
    near_bits = [bits_of(tile_offsets(offsets_ref, 0, t, 8), NEAR_SPAN) for t in tiles]
    wide_bits = [[bits_of(tile_offsets(offsets_ref, 1 + s, t, 8), MID_SPAN) for t in tiles] for s in range(wide)]
    chosen = {}
    for c, section in enumerate(sections):
        kept = SECTION // MID_SPAN
        for x in range(3):
            arrivals[c][x].wait()
            for t in tiles:
                lanes = tile_lanes(t)
                spread = stage[x, section, lanes].astype(F32)
                for g in range(kept):
                    for i in range(2):
                        at = g * MID_SPAN + 8 * i
                        single[x, t, pl.ds(c * kept + g + 8 * i * PITCH, 8, stride=PITCH), :] = spread[at : at + 8]
                near_parts = [[] for _ in range(NEAR_SPAN)]
                for chunk in range(c * kept // 8, (c + 1) * kept // 8):
                    block = [single[x, t, o * PITCH + 8 * chunk : o * PITCH + 8 * chunk + 8, :] for o in range(MID_SPAN)]
                    for a in range(NEAR_SPAN):
                        near_parts[a].append(pick(block[a * NEAR_SPAN : (a + 1) * NEAR_SPAN], near_bits[t]))
                    for s in range(wide):
                        picked = pick(block, wide_bits[s][t])
                        chosen[x, s, t, chunk] = pltpu.roll(picked, scale_lane(s), 1) if s else picked
                for a in range(NEAR_SPAN):
                    near_block = jnp.concatenate(near_parts[a], axis=0).astype(BF)
                    base = a * groups + c * kept
                    if x == 0:
                        near_q[base : base + kept, lanes] = near_block
                    else:
                        base += (x - 1) * near_rows
                        near[base : base + kept, lanes] = near_block
    leaving = flights([(near, near_out), (near_q, near_q_out)], out_sems.at[0])
    for h in range(H):
        travel = []
        for x in range(3):
            chunks = []
            for chunk in range(groups // 8):
                joined = jnp.zeros((8, TILE), F32)
                for s in range(wide):
                    for t in tiles_of(h):
                        low, high = max(h * HD, t * TILE), min((h + 1) * HD, (t + 1) * TILE)
                        turned = (lane - scale_lane(s)) & (TILE - 1)
                        hit = (turned >= low - t * TILE) & (turned < high - t * TILE)
                        joined = jnp.where(hit, chosen[x, s, t, chunk], joined)
                chunks.append(joined)
            travel += folded((lane - h * HD) & (TILE - 1), chunks)
        send[h] = jnp.concatenate(travel, axis=0).astype(BF)
        if h == H // 2 - 1:
            leaving += flights([(send.at[: H // 2], send_out.at[: H // 2])], out_sems.at[1])
    leaving += flights([(send.at[H // 2 :], send_out.at[H // 2 :])], out_sems.at[2])
    for copy in leaving:
        copy.wait()


def probabilities(scores):
    top = jnp.max(scores, axis=1, keepdims=True)
    return jnp.exp2((scores - top) * F32(SCALE * LOG2E)).astype(BF), top


def attend_half(q, k, v, stacked):
    count = q.shape[0]
    lane = lax.broadcasted_iota(jnp.int32, (1, TILE), 1)
    full_lane = lax.broadcasted_iota(jnp.int32, (count, TILE), 1)
    wide_lane = lax.broadcasted_iota(jnp.int32, (1, 2 * TILE), 1)
    num = [None] * 3
    den = [None] * 3
    top_tiles = [jnp.zeros((count, TILE), F32) for _ in range(3)]

    def add(into, tile, value):
        into[tile] = value if into[tile] is None else into[tile] + value

    def masked_query(h, start):
        return q[:, start : start + 2 * TILE] * inside(wide_lane, h * HD - start, (h + 1) * HD - start)

    def scores_of(left, start):
        right = k[:, start : start + 2 * TILE]
        return lax.dot_general(left, right, (((1,), (1,)), ((), ())), preferred_element_type=F32)

    starts = [0 if (h + 1) * HD <= 2 * TILE else TILE for h in range(HALF_HEADS)]
    ready = {}
    if stacked:
        for start in (0, TILE):
            members = [h for h in range(HALF_HEADS) if starts[h] == start]
            together = scores_of(jnp.concatenate([masked_query(h, start) for h in members], axis=0), start)
            for i, h in enumerate(members):
                ready[h] = together[i * count : (i + 1) * count]
    for h in range(HALF_HEADS):
        low, high = h * HD, (h + 1) * HD
        scores = ready[h] if stacked else scores_of(masked_query(h, starts[h]), starts[h])
        probs, top = probabilities(scores)
        first, last = low // TILE, (high - 1) // TILE
        inside_first = (full_lane >= low - first * TILE) & (full_lane < high - first * TILE)
        ones_first = inside(lane, low - first * TILE, high - first * TILE)
        v_first = v[:, first * TILE : (first + 1) * TILE] * ones_first
        if first == last:
            weights = jnp.concatenate([v_first, jnp.broadcast_to(ones_first, v_first.shape)], axis=1)
            result = jnp.dot(probs, weights, preferred_element_type=F32)
            add(num, first, result[:, :TILE])
            add(den, first, result[:, TILE:])
            top_tiles[first] = jnp.where(inside_first, top, top_tiles[first])
        else:
            inside_last = full_lane < high - last * TILE
            ones_last = inside(lane, 0, high - last * TILE)
            v_last = v[:, last * TILE : (last + 1) * TILE] * ones_last
            weights = jnp.concatenate([v_first + ones_last, v_last + ones_first], axis=1)
            result = jnp.dot(probs, weights, preferred_element_type=F32)
            left, right = result[:, :TILE], result[:, TILE:]
            zero = F32(0.0)
            add(num, first, jnp.where(inside_first, left, zero))
            add(den, first, jnp.where(inside_first, right, zero))
            add(num, last, jnp.where(inside_last, right, zero))
            add(den, last, jnp.where(inside_last, left, zero))
            top_tiles[first] = jnp.where(inside_first, top, top_tiles[first])
            top_tiles[last] = jnp.where(inside_last, top, top_tiles[last])
    branch = [n / d for n, d in zip(num, den)]
    lse = [t * F32(SCALE) + jnp.log(d) for t, d in zip(top_tiles, den)]
    return branch, lse


def local_kernel(q_ref, k_ref, v_ref, own_out, stage, own, in_sems, out_sems):
    arrivals = flights(
        [
            (ref.at[:, lanes_of(part)], stage.at[x, :, lanes_of(part)])
            for part in range(PARTS)
            for x, ref in enumerate((q_ref, k_ref, v_ref))
        ],
        in_sems,
    )
    leaving = []
    for part in range(PARTS):
        here = lanes_of(part)
        for x in range(3):
            arrivals[part * 3 + x].wait()
        branch_tiles, lse_tiles = attend_half(stage[0, :, here], stage[1, :, here], stage[2, :, here], False)
        for t in range(PART_TILES):
            own[0, part * PART_TILES + t] = branch_tiles[t]
            own[1, part * PART_TILES + t] = lse_tiles[t]
        tiles = range(part * PART_TILES, (part + 1) * PART_TILES)
        leaving += flights([(own.at[i, t], own_out.at[i, t]) for i in range(2) for t in tiles], out_sems.at[part])
    for copy in leaving:
        copy.wait()


def combine(branch_a, lse_a, branch_b, lse_b):
    high = jnp.maximum(lse_a, lse_b)
    weight_a = jnp.exp(lse_a - high)
    weight_b = jnp.exp(lse_b - high)
    total = weight_a + weight_b
    return (weight_a * branch_a + weight_b * branch_b) / total, high + jnp.log(total)


def near_kernel(wide, offsets_ref, q_ref, *refs):
    kv_refs, (own_ref, state_out) = refs[:NEAR_SPAN], refs[NEAR_SPAN : NEAR_SPAN + 2]
    q_stage, kv_stage, own, picked, kv_sems, own_sems, out_sems = refs[NEAR_SPAN + 2 :]
    near_rows = q_ref.shape[0]
    rows = own_ref.shape[2]
    groups = rows // MID_SPAN
    arrivals, own_arrivals, leaving = [], [], []
    for part in range(PARTS):
        here = lanes_of(part)
        pairs = [(q_ref.at[:, here], q_stage.at[:, here])]
        for i, ref in enumerate(kv_refs):
            for x in range(2):
                rows_x = slice(x * near_rows, (x + 1) * near_rows)
                rows_i = slice(i * near_rows, (i + 1) * near_rows)
                pairs.append((ref.at[rows_x, here], kv_stage.at[x, rows_i, here]))
        arrivals.append(flights(pairs, kv_sems.at[part]))
        tiles = range(part * PART_TILES, (part + 1) * PART_TILES)
        own_arrivals.append(
            flights([(own_ref.at[i, t], own.at[i, t]) for i in range(2) for t in tiles], own_sems.at[part])
        )
    for part in range(PARTS):
        here = lanes_of(part)
        for copy in arrivals[part]:
            copy.wait()
        near_branch, near_lse = attend_half(q_stage[:, here], kv_stage[0, :, here], kv_stage[1, :, here], True)
        for copy in own_arrivals[part]:
            copy.wait()
        for i in range(PART_TILES):
            t = part * PART_TILES + i
            offs = tile_offsets(offsets_ref, 0, t, 8)
            hits, bits = [offs == b for b in range(NEAR_SPAN)], bits_of(offs, NEAR_SPAN)
            wide_bits = [bits_of(tile_offsets(offsets_ref, 1 + s, t, 8), MID_SPAN) for s in range(wide)]
            for chunk in range(groups // 8):
                branch = [own[0, t, every(o, chunk), :] for o in range(MID_SPAN)]
                lse = [own[1, t, every(o, chunk), :] for o in range(MID_SPAN)]
                for a in range(NEAR_SPAN):
                    members = slice(a * NEAR_SPAN, (a + 1) * NEAR_SPAN)
                    span = slice(a * groups + chunk * 8, a * groups + (chunk + 1) * 8)
                    mixed, high = combine(
                        pick(branch[members], bits), pick(lse[members], bits), near_branch[i][span], near_lse[i][span]
                    )
                    for b, hit in enumerate(hits):
                        o = a * NEAR_SPAN + b
                        branch[o] = jnp.where(hit, mixed, branch[o])
                        lse[o] = jnp.where(hit, high, lse[o])
                        own[0, t, every(o, chunk), :] = branch[o]
                for s in range(wide):
                    for kind, blocks in enumerate((branch, lse)):
                        base = (2 * s + kind) * groups + chunk * 8
                        picked[t, base : base + 8] = pick(blocks, wide_bits[s])
        tiles = range(part * PART_TILES, (part + 1) * PART_TILES)
        pairs = [(own.at[0, t], state_out.at[t]) for t in tiles]
        pairs += [(picked.at[t], state_out.at[D // TILE + t, : 2 * wide * groups]) for t in tiles]
        leaving += flights(pairs, out_sems.at[part])
    for copy in leaving:
        copy.wait()


def owned_kernel(wide, recv_ref, back_out, back, out_sems):
    third = recv_ref.shape[1] // 3
    groups = third * 4 // 3
    head = lax.rem(lax.axis_index("seq"), H)
    lane = lax.broadcasted_iota(jnp.int32, (1, TILE), 1)
    row_place = (lane - head * HD) & (TILE - 1)
    chunk_place = (lax.broadcasted_iota(jnp.int32, (8, TILE), 1) - head * HD) & (TILE - 1)
    peers = [recv_ref[peer].astype(F32) for peer in range(MID_SPAN)]

    def rows_of(x):
        found = []
        for peer in peers:
            chunks = [peer[r : r + 8] for r in range(x * third, (x + 1) * third, 8)]
            found += unfolded(chunk_place, chunks)
        return jnp.concatenate(found, axis=0).astype(BF)

    q, k, v = (rows_of(x) for x in range(3))
    full_lane = lax.broadcasted_iota(jnp.int32, (q.shape[0], TILE), 1)
    place = (full_lane - head * HD) & (TILE - 1)
    num_den = None
    tops = jnp.zeros((q.shape[0], TILE), F32)
    for s in range(wide):
        low = scale_lane(s)
        columns = inside(row_place, low, low + HD)
        totals = columns + inside(row_place, STAT_LANE[s], STAT_LANE[s] + 3)
        weights = jnp.concatenate([v * columns, jnp.broadcast_to(totals, v.shape)], axis=1)
        half = q.shape[0] // 2
        blocks = []
        for rows in (slice(0, half), slice(half, 2 * half)):
            scores = lax.dot_general(q[rows] * columns, k, (((1,), (1,)), ((), ())), preferred_element_type=F32)
            probs, top = probabilities(scores)
            blocks.append((jnp.dot(probs, weights, preferred_element_type=F32), top))
        result, top = (jnp.concatenate(both, axis=0) for both in zip(*blocks))
        num_den = result if num_den is None else num_den + result
        tops = jnp.where((place >= STAT_LANE[s]) & (place < STAT_LANE[s] + 3), top, tops)
    den = num_den[:, TILE:]
    used = den > F32(0.0)
    den = jnp.where(used, den, F32(1.0))
    branch = num_den[:, :TILE] / den
    lse = tops * F32(SCALE) + jnp.log(den)
    first = lse.astype(BF).astype(F32)
    second = (lse - first).astype(BF).astype(F32)
    third = lse - first - second
    stat = place
    for s in range(wide):
        stat = jnp.where(place >= STAT_LANE[s], place - STAT_LANE[s], stat)
    split = jnp.where(stat == 0, first, jnp.where(stat == 1, second, third))
    split = jnp.where(used, split, F32(0.0))
    back[...] = jnp.where(place < wide * HD, branch, split).astype(BF)
    for copy in flights([(back, back_out)], out_sems):
        copy.wait()


def merge_kernel(wide, offsets_ref, back_ref, state_ref, out_ref, base, picked, out, in_sems, out_sems):
    rows = out_ref.shape[0]
    groups = rows // MID_SPAN
    arrivals = [
        flights(
            [(state_ref.at[D // TILE + t, : 2 * wide * groups], picked.at[t]), (state_ref.at[t], base.at[t])], in_sems.at[t]
        )
        for t in range(D // TILE)
    ]
    lane = lax.broadcasted_iota(jnp.int32, (1, TILE), 1)
    full_lane = lax.broadcasted_iota(jnp.int32, (groups, TILE), 1)
    row_in_16 = lax.broadcasted_iota(jnp.int32, (MID_SPAN, TILE), 0)
    ones = jnp.ones((TILE, TILE), BF)
    branches, lses = [], []
    for s in range(wide):
        turned, stats = [], []
        for h in range(H):
            mine = back_ref[h * groups : (h + 1) * groups, :]
            place = (lane - h * HD) & (TILE - 1)
            stats.append(mine * inside(place, STAT_LANE[s], STAT_LANE[s] + 3))
            single = mine.astype(F32)
            turned.append(pltpu.roll(single, TILE - scale_lane(s), 1) if s else single)
        branches.append(turned)
        lses.append(jnp.dot(jnp.concatenate(stats, axis=0), ones, preferred_element_type=F32))

    def by_tile(t, of_head):
        heads = list(heads_of(t))
        result = of_head(heads[0])
        for h in heads[1:]:
            result = jnp.where(full_lane >= h * HD - t * TILE, of_head(h), result)
        return result

    leaving = []
    for t in range(D // TILE):
        lanes = tile_lanes(t)
        arrivals[t][0].wait()
        offs, results = [], []
        for s in range(wide):
            start = 2 * s * groups
            branch, lse = picked[t, start : start + groups], picked[t, start + groups : start + 2 * groups]
            offs.append(tile_offsets(offsets_ref, 1 + s, t, MID_SPAN))
            for before, (other_branch, other_lse) in zip(offs, results):
                same = jnp.concatenate([before - offs[s]] * (groups // MID_SPAN), axis=0) == 0
                branch = jnp.where(same, other_branch, branch)
                lse = jnp.where(same, other_lse, lse)
            wide_branch = by_tile(t, lambda h: branches[s][h])
            wide_lse = by_tile(t, lambda h: lses[s][h * groups : (h + 1) * groups])
            results.append(combine(branch, lse, wide_branch, wide_lse))
        hits = [row_in_16 == off for off in offs]
        arrivals[t][1].wait()
        for g in range(groups):
            block = base[t, g * MID_SPAN : (g + 1) * MID_SPAN]
            for hit, (branch, _) in zip(hits, results):
                block = jnp.where(hit, jnp.broadcast_to(branch[g : g + 1], (MID_SPAN, TILE)), block)
            out[g * MID_SPAN : (g + 1) * MID_SPAN, lanes] = block.astype(BF)
        leaving += flights([(out.at[:, lanes], out_ref.at[:, lanes])], out_sems.at[t])
    for copy in leaving:
        copy.wait()


def far_by_gather(queries, key_rows, value_rows, choose, dilation):
    rows = queries.shape[0]

    def select(data):
        shaped = data.reshape(rows // dilation, dilation, H, HD)
        return jnp.take_along_axis(shaped, choose[None, None, :, None], axis=1)[:, 0]

    def gathered(data):
        flat = lax.all_gather(select(data).reshape(-1, D), "seq", axis=0, tiled=True)
        return flat.reshape(-1, H, HD)

    keys, values = gathered(key_rows), gathered(value_rows)
    scores = jnp.einsum("qhd,khd->hqk", select(queries), keys, preferred_element_type=F32) * SCALE
    top = jnp.max(scores, axis=-1, keepdims=True)
    expo = jnp.exp(scores - top)
    total = jnp.sum(expo, axis=-1)
    mixed = jnp.einsum("hqk,khd->qhd", expo.astype(BF), values, preferred_element_type=F32)
    mixed = mixed / jnp.transpose(total)[:, :, None]
    lse = jnp.transpose(top[..., 0] + jnp.log(total))
    selected = jnp.arange(dilation)[:, None] == choose[None, :]
    full_mixed = jnp.where(selected[None, :, :, None], mixed[:, None], F32(0.0)).reshape(rows, D)
    full_lse = jnp.where(selected[None], lse[:, None], F32(-1e30)).reshape(rows, H)
    full_lse = jnp.repeat(full_lse, HD, axis=1)

    def tiled(data):
        return data.reshape(rows, D // TILE, TILE).swapaxes(0, 1)

    return tiled(full_mixed), tiled(full_lse)


def exchange(blocks):
    count = lax.axis_size("seq")
    teams = None
    if count != MID_SPAN:
        teams = [[first + i for i in range(MID_SPAN)] for first in range(0, count, MID_SPAN)]
    return lax.all_to_all(blocks, "seq", 0, 0, axis_index_groups=teams, tiled=True)


def shards(queries, key_rows, value_rows, offsets):
    rows = queries.shape[0]
    count = lax.axis_size("seq")
    wide = 2 if count == MID_SPAN else 1
    groups = rows // MID_SPAN
    near_rows = rows // NEAR_SPAN
    send_shape = (H, 3 * groups * 3 // 4, TILE)
    back_rows = H * groups
    smem = pl.BlockSpec(memory_space=pltpu.SMEM)
    vmem = pl.BlockSpec(memory_space=pltpu.VMEM)
    hbm = pl.BlockSpec(memory_space=pltpu.HBM)
    shape = jax.ShapeDtypeStruct

    def sems(*count):
        return pltpu.SemaphoreType.DMA(count)

    near_q, near_kv, send = pl.pallas_call(
        functools.partial(prep_kernel, wide),
        out_shape=(
            shape((near_rows, D), BF),
            shape((2 * near_rows, D), BF),
            shape(send_shape, BF),
        ),
        in_specs=[smem, hbm, hbm, hbm],
        out_specs=(hbm, hbm, hbm),
        scratch_shapes=[
            pltpu.VMEM((3, rows, D), BF),
            pltpu.VMEM((3, D // TILE, MID_SPAN * PITCH, TILE), F32),
            pltpu.VMEM((near_rows, D), BF),
            pltpu.VMEM((2 * near_rows, D), BF),
            pltpu.VMEM(send_shape, BF),
            sems(rows // SECTION, 3),
            sems(3, 2),
        ],
        compiler_params=params(),
        cost_estimate=cost(6 * rows * D, 10 * rows * D),
        name="prep",
    )(offsets, queries, key_rows, value_rows)

    near_side = from_partner(near_kv, "seq", 2)
    near_core = from_partner(near_kv, "seq", 1)
    recv = exchange(send)

    tiled = (2, D // TILE, rows, TILE)
    own = pl.pallas_call(
        local_kernel,
        out_shape=shape(tiled, F32),
        in_specs=[hbm] * 3,
        out_specs=hbm,
        scratch_shapes=[pltpu.VMEM((3, rows, D), BF), pltpu.VMEM(tiled, F32), sems(PARTS * 3), sems(PARTS, 2 * PART_TILES)],
        compiler_params=params(),
        cost_estimate=cost(16 * rows * rows * H * 256, 14 * rows * D, rows * rows * H),
        name="local",
    )(queries, key_rows, value_rows)
    own, recv, near_side = lax.optimization_barrier((own, recv, near_side))

    near_both = from_partner(near_side, "seq", 1)
    back = pl.pallas_call(
        functools.partial(owned_kernel, wide),
        out_shape=shape((back_rows, TILE), BF),
        in_specs=[vmem],
        out_specs=hbm,
        scratch_shapes=[pltpu.VMEM((back_rows, TILE), BF), sems(1)],
        compiler_params=params(OWNED_BYTES),
        cost_estimate=cost(4 * wide * rows * rows * 256, 4 * rows * D, wide * rows * rows),
        name="owned",
    )(recv)
    back = exchange(back)

    if wide == 1:
        far_branch, far_lse = far_by_gather(queries, key_rows, value_rows, offsets[2], count)
        own = jnp.stack(combine(own[0], own[1], far_branch, far_lse))
    state = pl.pallas_call(
        functools.partial(near_kernel, wide),
        out_shape=shape((12 * D // TILE, rows, TILE), F32),
        in_specs=[smem] + [hbm] * (2 + NEAR_SPAN),
        out_specs=hbm,
        scratch_shapes=[
            pltpu.VMEM((near_rows, D), BF),
            pltpu.VMEM((2, NEAR_SPAN * near_rows, D), BF),
            pltpu.VMEM(tiled, F32),
            pltpu.VMEM((D // TILE, 2 * wide * groups, TILE), F32),
            sems(PARTS, 1 + 2 * NEAR_SPAN),
            sems(PARTS, 2 * PART_TILES),
            sems(PARTS, 2 * PART_TILES),
        ],
        compiler_params=params(),
        cost_estimate=cost(4 * near_rows * rows * H * 256, 8 * rows * D, near_rows * rows * H),
        name="near",
    )(offsets, near_q, near_kv, near_core, near_side, near_both, own)
    state, back = lax.optimization_barrier((state, back))

    return pl.pallas_call(
        functools.partial(merge_kernel, wide),
        out_shape=shape((rows, D), BF),
        in_specs=[smem, vmem, hbm],
        out_specs=hbm,
        scratch_shapes=[
            pltpu.VMEM((D // TILE, rows, TILE), F32),
            pltpu.VMEM((D // TILE, 2 * wide * groups, TILE), F32),
            pltpu.VMEM((rows, D), BF),
            sems(D // TILE, 2),
            sems(D // TILE, 1),
        ],
        compiler_params=params(SMALL_BYTES),
        cost_estimate=cost(2 * rows * rows * D, 14 * rows * D),
        name="merge",
    )(offsets, back, state)


def solution(mesh):
    in_specs = (
        P(("slides", "seq"), None),
        P(("slides", "seq"), None),
        P(("slides", "seq"), None),
        P(),
    )
    out_specs = P(("slides", "seq"), None)
    return jax.shard_map(shards, mesh=mesh, in_specs=in_specs, out_specs=out_specs, check_vma=False)
```

```python
import functools

import jax
import jax.numpy as jnp
from jax import lax
from jax.experimental import pallas as pl
from jax.experimental.pallas import tpu as pltpu
from jax.sharding import PartitionSpec as P

H = 16
HD = 48
D = 768
NEAR_SPAN = 4
MID_SPAN = 16
HALF = 384
TILE = 128
HALF_HEADS = HALF // HD
PARTS = D // HALF
PART_TILES = HALF // TILE
STAT_LANE = (2 * HD, 2 * HD + 16)
SPARE = TILE - 2 * HD
SECTION = 256
PITCH = 36
SCALE = HD ** (-0.5)
LOG2E = 1.4426950408889634
VMEM_BYTES = 63 * 1024 * 1024
SMALL_BYTES = 48 * 1024 * 1024
OWNED_BYTES = 32 * 1024 * 1024
BF = jnp.bfloat16
F32 = jnp.float32


def from_partner(block, axis, flip):
    count = lax.axis_size(axis)
    return lax.ppermute(block, axis, [(i, i ^ flip) for i in range(count)])


def params(limit=VMEM_BYTES):
    return pltpu.CompilerParams(vmem_limit_bytes=limit)


def cost(flops, moved, exps=0):
    return pl.CostEstimate(flops=flops, bytes_accessed=moved, transcendentals=exps)


def tile_offsets(offsets_ref, scale, tile, rows):
    lane = lax.broadcasted_iota(jnp.int32, (rows, TILE), 1)
    heads = list(heads_of(tile))
    result = jnp.full((rows, TILE), offsets_ref[scale, heads[0]], jnp.int32)
    for h in heads[1:]:
        result = jnp.where(lane >= h * HD - tile * TILE, offsets_ref[scale, h], result)
    return result


def inside(lane, low, high):
    return jnp.where((lane >= low) & (lane < high), F32(1.0), F32(0.0)).astype(BF)


def heads_of(tile):
    return range(tile * TILE // HD, ((tile + 1) * TILE - 1) // HD + 1)


def tiles_of(head):
    return range(head * HD // TILE, ((head + 1) * HD - 1) // TILE + 1)


def every(first, chunk):
    return pl.ds(first + MID_SPAN * 8 * chunk, 8, stride=MID_SPAN)


def bits_of(offs, count):
    return [(offs & (1 << k)) != 0 for k in range(count.bit_length() - 1)]


def pick(blocks, bits):
    for bit in bits:
        blocks = [jnp.where(bit, high, low) for low, high in zip(blocks[::2], blocks[1::2])]
    return blocks[0]


def tile_lanes(tile):
    return slice(tile * TILE, (tile + 1) * TILE)


def lanes_of(part):
    return slice(part * HALF, (part + 1) * HALF)


def flights(pairs, sems):
    copies = [pltpu.make_async_copy(src, dst, sems.at[i]) for i, (src, dst) in enumerate(pairs)]
    for copy in copies:
        copy.start()
    return copies


def scale_lane(scale):
    return scale * HD


def spare_turn(piece):
    return (2 * HD - piece * SPARE) % TILE


def folded(place, chunks):
    result = []
    for first in range(0, len(chunks), 4):
        last = chunks[first + 3]
        for piece in range(3):
            moved = pltpu.roll(last, spare_turn(piece), 1) if spare_turn(piece) else last
            result.append(jnp.where(place < 2 * HD, chunks[first + piece], moved))
    return result


def unfolded(place, chunks):
    result = []
    for first in range(0, len(chunks), 3):
        last = None
        for piece in range(3):
            turn = (TILE - spare_turn(piece)) % TILE
            moved = pltpu.roll(chunks[first + piece], turn, 1) if turn else chunks[first + piece]
            last = moved if last is None else jnp.where(place >= piece * SPARE, moved, last)
        result += chunks[first : first + 3] + [last]
    return result


def prep_kernel(
    wide, offsets_ref, q_ref, k_ref, v_ref, near_q_out, near_out, send_out,
    stage, single, near_q, near, send, in_sems, out_sems,
):
    rows = q_ref.shape[0]
    groups = rows // MID_SPAN
    near_rows = rows // NEAR_SPAN
    tiles = range(D // TILE)
    sections = [slice(c * SECTION, (c + 1) * SECTION) for c in range(rows // SECTION)]
    arrivals = [
        flights([(ref.at[section], stage.at[x, section]) for x, ref in enumerate((q_ref, k_ref, v_ref))], in_sems.at[c])
        for c, section in enumerate(sections)
    ]
    lane = lax.broadcasted_iota(jnp.int32, (8, TILE), 1)
    near_bits = [bits_of(tile_offsets(offsets_ref, 0, t, 8), NEAR_SPAN) for t in tiles]
    wide_bits = [[bits_of(tile_offsets(offsets_ref, 1 + s, t, 8), MID_SPAN) for t in tiles] for s in range(wide)]
    chosen = {}
    for c, section in enumerate(sections):
        kept = SECTION // MID_SPAN
        for x in range(3):
            arrivals[c][x].wait()
            for t in tiles:
                lanes = tile_lanes(t)
                spread = stage[x, section, lanes].astype(F32)
                for g in range(kept):
                    for i in range(2):
                        at = g * MID_SPAN + 8 * i
                        single[x, t, pl.ds(c * kept + g + 8 * i * PITCH, 8, stride=PITCH), :] = spread[at : at + 8]
                near_parts = [[] for _ in range(NEAR_SPAN)]
                for chunk in range(c * kept // 8, (c + 1) * kept // 8):
                    block = [single[x, t, o * PITCH + 8 * chunk : o * PITCH + 8 * chunk + 8, :] for o in range(MID_SPAN)]
                    for a in range(NEAR_SPAN):
                        near_parts[a].append(pick(block[a * NEAR_SPAN : (a + 1) * NEAR_SPAN], near_bits[t]))
                    for s in range(wide):
                        picked = pick(block, wide_bits[s][t])
                        chosen[x, s, t, chunk] = pltpu.roll(picked, scale_lane(s), 1) if s else picked
                for a in range(NEAR_SPAN):
                    near_block = jnp.concatenate(near_parts[a], axis=0).astype(BF)
                    base = a * groups + c * kept
                    if x == 0:
                        near_q[base : base + kept, lanes] = near_block
                    else:
                        base += (x - 1) * near_rows
                        near[base : base + kept, lanes] = near_block
    leaving = flights([(near, near_out), (near_q, near_q_out)], out_sems.at[0])
    for h in range(H):
        travel = []
        for x in range(3):
            chunks = []
            for chunk in range(groups // 8):
                joined = jnp.zeros((8, TILE), F32)
                for s in range(wide):
                    for t in tiles_of(h):
                        low, high = max(h * HD, t * TILE), min((h + 1) * HD, (t + 1) * TILE)
                        turned = (lane - scale_lane(s)) & (TILE - 1)
                        hit = (turned >= low - t * TILE) & (turned < high - t * TILE)
                        joined = jnp.where(hit, chosen[x, s, t, chunk], joined)
                chunks.append(joined)
            travel += folded((lane - h * HD) & (TILE - 1), chunks)
        send[h] = jnp.concatenate(travel, axis=0).astype(BF)
        if h == H // 2 - 1:
            leaving += flights([(send.at[: H // 2], send_out.at[: H // 2])], out_sems.at[1])
    leaving += flights([(send.at[H // 2 :], send_out.at[H // 2 :])], out_sems.at[2])
    for copy in leaving:
        copy.wait()


def probabilities(scores):
    top = jnp.max(scores, axis=1, keepdims=True)
    return jnp.exp2((scores - top) * F32(SCALE * LOG2E)).astype(BF), top


def attend_half(q, k, v, stacked):
    count = q.shape[0]
    lane = lax.broadcasted_iota(jnp.int32, (1, TILE), 1)
    full_lane = lax.broadcasted_iota(jnp.int32, (count, TILE), 1)
    wide_lane = lax.broadcasted_iota(jnp.int32, (1, 2 * TILE), 1)
    num = [None] * 3
    den = [None] * 3
    top_tiles = [jnp.zeros((count, TILE), F32) for _ in range(3)]

    def add(into, tile, value):
        into[tile] = value if into[tile] is None else into[tile] + value

    def masked_query(h, start):
        return q[:, start : start + 2 * TILE] * inside(wide_lane, h * HD - start, (h + 1) * HD - start)

    def scores_of(left, start):
        right = k[:, start : start + 2 * TILE]
        return lax.dot_general(left, right, (((1,), (1,)), ((), ())), preferred_element_type=F32)

    starts = [0 if (h + 1) * HD <= 2 * TILE else TILE for h in range(HALF_HEADS)]
    ready = {}
    if stacked:
        for start in (0, TILE):
            members = [h for h in range(HALF_HEADS) if starts[h] == start]
            together = scores_of(jnp.concatenate([masked_query(h, start) for h in members], axis=0), start)
            for i, h in enumerate(members):
                ready[h] = together[i * count : (i + 1) * count]
    for h in range(HALF_HEADS):
        low, high = h * HD, (h + 1) * HD
        scores = ready[h] if stacked else scores_of(masked_query(h, starts[h]), starts[h])
        probs, top = probabilities(scores)
        first, last = low // TILE, (high - 1) // TILE
        inside_first = (full_lane >= low - first * TILE) & (full_lane < high - first * TILE)
        ones_first = inside(lane, low - first * TILE, high - first * TILE)
        v_first = v[:, first * TILE : (first + 1) * TILE] * ones_first
        if first == last:
            weights = jnp.concatenate([v_first, jnp.broadcast_to(ones_first, v_first.shape)], axis=1)
            result = jnp.dot(probs, weights, preferred_element_type=F32)
            add(num, first, result[:, :TILE])
            add(den, first, result[:, TILE:])
            top_tiles[first] = jnp.where(inside_first, top, top_tiles[first])
        else:
            inside_last = full_lane < high - last * TILE
            ones_last = inside(lane, 0, high - last * TILE)
            v_last = v[:, last * TILE : (last + 1) * TILE] * ones_last
            weights = jnp.concatenate([v_first + ones_last, v_last + ones_first], axis=1)
            result = jnp.dot(probs, weights, preferred_element_type=F32)
            left, right = result[:, :TILE], result[:, TILE:]
            zero = F32(0.0)
            add(num, first, jnp.where(inside_first, left, zero))
            add(den, first, jnp.where(inside_first, right, zero))
            add(num, last, jnp.where(inside_last, right, zero))
            add(den, last, jnp.where(inside_last, left, zero))
            top_tiles[first] = jnp.where(inside_first, top, top_tiles[first])
            top_tiles[last] = jnp.where(inside_last, top, top_tiles[last])
    branch = [n / d for n, d in zip(num, den)]
    lse = [t * F32(SCALE) + jnp.log(d) for t, d in zip(top_tiles, den)]
    return branch, lse


def local_kernel(q_ref, k_ref, v_ref, own_out, stage, own, in_sems, out_sems):
    arrivals = flights(
        [
            (ref.at[:, lanes_of(part)], stage.at[x, :, lanes_of(part)])
            for part in range(PARTS)
            for x, ref in enumerate((q_ref, k_ref, v_ref))
        ],
        in_sems,
    )
    leaving = []
    for part in range(PARTS):
        here = lanes_of(part)
        for x in range(3):
            arrivals[part * 3 + x].wait()
        branch_tiles, lse_tiles = attend_half(stage[0, :, here], stage[1, :, here], stage[2, :, here], False)
        for t in range(PART_TILES):
            own[0, part * PART_TILES + t] = branch_tiles[t]
            own[1, part * PART_TILES + t] = lse_tiles[t]
        tiles = range(part * PART_TILES, (part + 1) * PART_TILES)
        leaving += flights([(own.at[i, t], own_out.at[i, t]) for i in range(2) for t in tiles], out_sems.at[part])
    for copy in leaving:
        copy.wait()


def combine(branch_a, lse_a, branch_b, lse_b):
    high = jnp.maximum(lse_a, lse_b)
    weight_a = jnp.exp(lse_a - high)
    weight_b = jnp.exp(lse_b - high)
    total = weight_a + weight_b
    return (weight_a * branch_a + weight_b * branch_b) / total, high + jnp.log(total)


def near_kernel(wide, offsets_ref, q_ref, *refs):
    kv_refs, (own_ref, base_out, picked_out) = refs[:NEAR_SPAN], refs[NEAR_SPAN : NEAR_SPAN + 3]
    q_stage, kv_stage, own, base, picked, kv_sems, own_sems, out_sems = refs[NEAR_SPAN + 3 :]
    near_rows = q_ref.shape[0]
    rows = own_ref.shape[2]
    groups = rows // MID_SPAN
    arrivals, own_arrivals, leaving = [], [], []
    for part in range(PARTS):
        here = lanes_of(part)
        pairs = [(q_ref.at[:, here], q_stage.at[:, here])]
        for i, ref in enumerate(kv_refs):
            for x in range(2):
                rows_x = slice(x * near_rows, (x + 1) * near_rows)
                rows_i = slice(i * near_rows, (i + 1) * near_rows)
                pairs.append((ref.at[rows_x, here], kv_stage.at[x, rows_i, here]))
        arrivals.append(flights(pairs, kv_sems.at[part]))
        tiles = range(part * PART_TILES, (part + 1) * PART_TILES)
        own_arrivals.append(
            flights([(own_ref.at[i, t], own.at[i, t]) for i in range(2) for t in tiles], own_sems.at[part])
        )
    for part in range(PARTS):
        here = lanes_of(part)
        for copy in arrivals[part]:
            copy.wait()
        near_branch, near_lse = attend_half(q_stage[:, here], kv_stage[0, :, here], kv_stage[1, :, here], True)
        for copy in own_arrivals[part]:
            copy.wait()
        for i in range(PART_TILES):
            t = part * PART_TILES + i
            offs = tile_offsets(offsets_ref, 0, t, 8)
            hits, bits = [offs == b for b in range(NEAR_SPAN)], bits_of(offs, NEAR_SPAN)
            wide_bits = [bits_of(tile_offsets(offsets_ref, 1 + s, t, 8), MID_SPAN) for s in range(wide)]
            for chunk in range(groups // 8):
                branch = [own[0, t, every(o, chunk), :] for o in range(MID_SPAN)]
                lse = [own[1, t, every(o, chunk), :] for o in range(MID_SPAN)]
                for a in range(NEAR_SPAN):
                    members = slice(a * NEAR_SPAN, (a + 1) * NEAR_SPAN)
                    span = slice(a * groups + chunk * 8, a * groups + (chunk + 1) * 8)
                    mixed, high = combine(
                        pick(branch[members], bits), pick(lse[members], bits), near_branch[i][span], near_lse[i][span]
                    )
                    for b, hit in enumerate(hits):
                        o = a * NEAR_SPAN + b
                        branch[o] = jnp.where(hit, mixed, branch[o])
                        lse[o] = jnp.where(hit, high, lse[o])
                        own[0, t, every(o, chunk), :] = branch[o]
                for s in range(wide):
                    for kind, blocks in enumerate((branch, lse)):
                        at = (2 * s + kind) * groups + chunk * 8
                        picked[t, at : at + 8] = pick(blocks, wide_bits[s])
            base[t] = own[0, t].astype(BF)
        tiles = range(part * PART_TILES, (part + 1) * PART_TILES)
        pairs = [(base.at[t], base_out.at[t]) for t in tiles]
        pairs += [(picked.at[t], picked_out.at[t]) for t in tiles]
        leaving += flights(pairs, out_sems.at[part])
    for copy in leaving:
        copy.wait()


def owned_kernel(wide, recv_ref, back_out, back, out_sems):
    third = recv_ref.shape[1] // 3
    groups = third * 4 // 3
    head = lax.rem(lax.axis_index("seq"), H)
    lane = lax.broadcasted_iota(jnp.int32, (1, TILE), 1)
    row_place = (lane - head * HD) & (TILE - 1)
    chunk_place = (lax.broadcasted_iota(jnp.int32, (8, TILE), 1) - head * HD) & (TILE - 1)
    peers = [recv_ref[peer].astype(F32) for peer in range(MID_SPAN)]

    def rows_of(x):
        found = []
        for peer in peers:
            chunks = [peer[r : r + 8] for r in range(x * third, (x + 1) * third, 8)]
            found += unfolded(chunk_place, chunks)
        return jnp.concatenate(found, axis=0).astype(BF)

    q, k, v = (rows_of(x) for x in range(3))
    full_lane = lax.broadcasted_iota(jnp.int32, (q.shape[0], TILE), 1)
    place = (full_lane - head * HD) & (TILE - 1)
    num_den = None
    tops = jnp.zeros((q.shape[0], TILE), F32)
    for s in range(wide):
        low = scale_lane(s)
        columns = inside(row_place, low, low + HD)
        totals = columns + inside(row_place, STAT_LANE[s], STAT_LANE[s] + 3)
        weights = jnp.concatenate([v * columns, jnp.broadcast_to(totals, v.shape)], axis=1)
        half = q.shape[0] // 2
        blocks = []
        for rows in (slice(0, half), slice(half, 2 * half)):
            scores = lax.dot_general(q[rows] * columns, k, (((1,), (1,)), ((), ())), preferred_element_type=F32)
            probs, top = probabilities(scores)
            blocks.append((jnp.dot(probs, weights, preferred_element_type=F32), top))
        result, top = (jnp.concatenate(both, axis=0) for both in zip(*blocks))
        num_den = result if num_den is None else num_den + result
        tops = jnp.where((place >= STAT_LANE[s]) & (place < STAT_LANE[s] + 3), top, tops)
    den = num_den[:, TILE:]
    used = den > F32(0.0)
    den = jnp.where(used, den, F32(1.0))
    branch = num_den[:, :TILE] / den
    lse = tops * F32(SCALE) + jnp.log(den)
    first = lse.astype(BF).astype(F32)
    second = (lse - first).astype(BF).astype(F32)
    third = lse - first - second
    stat = place
    for s in range(wide):
        stat = jnp.where(place >= STAT_LANE[s], place - STAT_LANE[s], stat)
    split = jnp.where(stat == 0, first, jnp.where(stat == 1, second, third))
    split = jnp.where(used, split, F32(0.0))
    back[...] = jnp.where(place < wide * HD, branch, split).astype(BF)
    for copy in flights([(back, back_out)], out_sems):
        copy.wait()


def merge_kernel(wide, offsets_ref, back_ref, base_ref, picked_ref, out_ref, base, picked, out, in_sems, out_sems):
    rows = out_ref.shape[0]
    groups = rows // MID_SPAN
    arrivals = [
        flights(
            [(picked_ref.at[t], picked.at[t]), (base_ref.at[t], base.at[t])], in_sems.at[t]
        )
        for t in range(D // TILE)
    ]
    lane = lax.broadcasted_iota(jnp.int32, (1, TILE), 1)
    full_lane = lax.broadcasted_iota(jnp.int32, (groups, TILE), 1)
    row_in_16 = lax.broadcasted_iota(jnp.int32, (MID_SPAN, TILE), 0)
    ones = jnp.ones((TILE, TILE), BF)
    branches, lses = [], []
    for s in range(wide):
        turned, stats = [], []
        for h in range(H):
            mine = back_ref[h * groups : (h + 1) * groups, :]
            place = (lane - h * HD) & (TILE - 1)
            stats.append(mine * inside(place, STAT_LANE[s], STAT_LANE[s] + 3))
            single = mine.astype(F32)
            turned.append(pltpu.roll(single, TILE - scale_lane(s), 1) if s else single)
        branches.append(turned)
        lses.append(jnp.dot(jnp.concatenate(stats, axis=0), ones, preferred_element_type=F32))

    def by_tile(t, of_head):
        heads = list(heads_of(t))
        result = of_head(heads[0])
        for h in heads[1:]:
            result = jnp.where(full_lane >= h * HD - t * TILE, of_head(h), result)
        return result

    leaving = []
    for t in range(D // TILE):
        lanes = tile_lanes(t)
        arrivals[t][0].wait()
        offs, results = [], []
        for s in range(wide):
            start = 2 * s * groups
            branch, lse = picked[t, start : start + groups], picked[t, start + groups : start + 2 * groups]
            offs.append(tile_offsets(offsets_ref, 1 + s, t, MID_SPAN))
            for before, (other_branch, other_lse) in zip(offs, results):
                same = jnp.concatenate([before - offs[s]] * (groups // MID_SPAN), axis=0) == 0
                branch = jnp.where(same, other_branch, branch)
                lse = jnp.where(same, other_lse, lse)
            wide_branch = by_tile(t, lambda h: branches[s][h])
            wide_lse = by_tile(t, lambda h: lses[s][h * groups : (h + 1) * groups])
            results.append(combine(branch, lse, wide_branch, wide_lse))
        hits = [row_in_16 == off for off in offs]
        arrivals[t][1].wait()
        for g in range(groups):
            block = base[t, g * MID_SPAN : (g + 1) * MID_SPAN].astype(F32)
            for hit, (branch, _) in zip(hits, results):
                block = jnp.where(hit, jnp.broadcast_to(branch[g : g + 1], (MID_SPAN, TILE)), block)
            out[g * MID_SPAN : (g + 1) * MID_SPAN, lanes] = block.astype(BF)
        leaving += flights([(out.at[:, lanes], out_ref.at[:, lanes])], out_sems.at[t])
    for copy in leaving:
        copy.wait()


def far_by_gather(queries, key_rows, value_rows, choose, dilation):
    rows = queries.shape[0]

    def select(data):
        shaped = data.reshape(rows // dilation, dilation, H, HD)
        return jnp.take_along_axis(shaped, choose[None, None, :, None], axis=1)[:, 0]

    def gathered(data):
        flat = lax.all_gather(select(data).reshape(-1, D), "seq", axis=0, tiled=True)
        return flat.reshape(-1, H, HD)

    keys, values = gathered(key_rows), gathered(value_rows)
    scores = jnp.einsum("qhd,khd->hqk", select(queries), keys, preferred_element_type=F32) * SCALE
    top = jnp.max(scores, axis=-1, keepdims=True)
    expo = jnp.exp(scores - top)
    total = jnp.sum(expo, axis=-1)
    mixed = jnp.einsum("hqk,khd->qhd", expo.astype(BF), values, preferred_element_type=F32)
    mixed = mixed / jnp.transpose(total)[:, :, None]
    lse = jnp.transpose(top[..., 0] + jnp.log(total))
    selected = jnp.arange(dilation)[:, None] == choose[None, :]
    full_mixed = jnp.where(selected[None, :, :, None], mixed[:, None], F32(0.0)).reshape(rows, D)
    full_lse = jnp.where(selected[None], lse[:, None], F32(-1e30)).reshape(rows, H)
    full_lse = jnp.repeat(full_lse, HD, axis=1)

    def tiled(data):
        return data.reshape(rows, D // TILE, TILE).swapaxes(0, 1)

    return tiled(full_mixed), tiled(full_lse)


def exchange(blocks):
    count = lax.axis_size("seq")
    teams = None
    if count != MID_SPAN:
        teams = [[first + i for i in range(MID_SPAN)] for first in range(0, count, MID_SPAN)]
    return lax.all_to_all(blocks, "seq", 0, 0, axis_index_groups=teams, tiled=True)


def shards(queries, key_rows, value_rows, offsets):
    rows = queries.shape[0]
    count = lax.axis_size("seq")
    wide = 2 if count == MID_SPAN else 1
    groups = rows // MID_SPAN
    near_rows = rows // NEAR_SPAN
    send_shape = (H, 3 * groups * 3 // 4, TILE)
    back_rows = H * groups
    smem = pl.BlockSpec(memory_space=pltpu.SMEM)
    vmem = pl.BlockSpec(memory_space=pltpu.VMEM)
    hbm = pl.BlockSpec(memory_space=pltpu.HBM)
    shape = jax.ShapeDtypeStruct

    def sems(*count):
        return pltpu.SemaphoreType.DMA(count)

    near_q, near_kv, send = pl.pallas_call(
        functools.partial(prep_kernel, wide),
        out_shape=(
            shape((near_rows, D), BF),
            shape((2 * near_rows, D), BF),
            shape(send_shape, BF),
        ),
        in_specs=[smem, hbm, hbm, hbm],
        out_specs=(hbm, hbm, hbm),
        scratch_shapes=[
            pltpu.VMEM((3, rows, D), BF),
            pltpu.VMEM((3, D // TILE, MID_SPAN * PITCH, TILE), F32),
            pltpu.VMEM((near_rows, D), BF),
            pltpu.VMEM((2 * near_rows, D), BF),
            pltpu.VMEM(send_shape, BF),
            sems(rows // SECTION, 3),
            sems(3, 2),
        ],
        compiler_params=params(),
        cost_estimate=cost(6 * rows * D, 10 * rows * D),
        name="prep",
    )(offsets, queries, key_rows, value_rows)

    near_side = from_partner(near_kv, "seq", 2)
    near_core = from_partner(near_kv, "seq", 1)
    recv = exchange(send)

    tiled = (2, D // TILE, rows, TILE)
    own = pl.pallas_call(
        local_kernel,
        out_shape=shape(tiled, F32),
        in_specs=[hbm] * 3,
        out_specs=hbm,
        scratch_shapes=[pltpu.VMEM((3, rows, D), BF), pltpu.VMEM(tiled, F32), sems(PARTS * 3), sems(PARTS, 2 * PART_TILES)],
        compiler_params=params(),
        cost_estimate=cost(16 * rows * rows * H * 256, 14 * rows * D, rows * rows * H),
        name="local",
    )(queries, key_rows, value_rows)
    own, recv, near_side = lax.optimization_barrier((own, recv, near_side))

    near_both = from_partner(near_side, "seq", 1)
    back = pl.pallas_call(
        functools.partial(owned_kernel, wide),
        out_shape=shape((back_rows, TILE), BF),
        in_specs=[vmem],
        out_specs=hbm,
        scratch_shapes=[pltpu.VMEM((back_rows, TILE), BF), sems(1)],
        compiler_params=params(OWNED_BYTES),
        cost_estimate=cost(4 * wide * rows * rows * 256, 4 * rows * D, wide * rows * rows),
        name="owned",
    )(recv)
    back = exchange(back)

    if wide == 1:
        far_branch, far_lse = far_by_gather(queries, key_rows, value_rows, offsets[2], count)
        own = jnp.stack(combine(own[0], own[1], far_branch, far_lse))
    base, picked = pl.pallas_call(
        functools.partial(near_kernel, wide),
        out_shape=(
            shape((24 * D // TILE, rows, TILE), BF),
            shape((48 * D // TILE, 2 * wide * groups, TILE), F32),
        ),
        in_specs=[smem] + [hbm] * (2 + NEAR_SPAN),
        out_specs=(hbm, hbm),
        scratch_shapes=[
            pltpu.VMEM((near_rows, D), BF),
            pltpu.VMEM((2, NEAR_SPAN * near_rows, D), BF),
            pltpu.VMEM(tiled, F32),
            pltpu.VMEM((D // TILE, rows, TILE), BF),
            pltpu.VMEM((D // TILE, 2 * wide * groups, TILE), F32),
            sems(PARTS, 1 + 2 * NEAR_SPAN),
            sems(PARTS, 2 * PART_TILES),
            sems(PARTS, 2 * PART_TILES),
        ],
        compiler_params=params(),
        cost_estimate=cost(4 * near_rows * rows * H * 256, 8 * rows * D, near_rows * rows * H),
        name="near",
    )(offsets, near_q, near_kv, near_core, near_side, near_both, own)
    base, picked, back = lax.optimization_barrier((base, picked, back))

    return pl.pallas_call(
        functools.partial(merge_kernel, wide),
        out_shape=shape((rows, D), BF),
        in_specs=[smem, vmem, hbm, hbm],
        out_specs=hbm,
        scratch_shapes=[
            pltpu.VMEM((D // TILE, rows, TILE), BF),
            pltpu.VMEM((D // TILE, 2 * wide * groups, TILE), F32),
            pltpu.VMEM((rows, D), BF),
            sems(D // TILE, 2),
            sems(D // TILE, 1),
        ],
        compiler_params=params(SMALL_BYTES),
        cost_estimate=cost(2 * rows * rows * D, 14 * rows * D),
        name="merge",
    )(offsets, back, base, picked)


def solution(mesh):
    in_specs = (
        P(("slides", "seq"), None),
        P(("slides", "seq"), None),
        P(("slides", "seq"), None),
        P(),
    )
    out_specs = P(("slides", "seq"), None)
    return jax.shard_map(shards, mesh=mesh, in_specs=in_specs, out_specs=out_specs, check_vma=False)
```
